512 devices in a mesh: task: 16 (over z), shard: 32 (over x, y, core).
Axes of the slice: x: 4, y: 4, z: 16, core: 2. Of those that a mesh axis runs over, the one named last changes fastest.
Arguments:
- inputs: bfloat16 [4608, 512], P('shard'), may hold values from -6 to 6
- cotangent: bfloat16 [16, 4608, 512], P('task', 'shard'), as said below
- routes: int32 [16, 512], P('task'), may hold values from 0 to 15
- adapter_down_factor: bfloat16 [4608, 512], P('shard'), may hold values from -0.09375 to 0.09375
- adapter_up_factor: bfloat16 [4608, 512], P('shard'), may hold values from -0.09375 to 0.09375
- order: int32 [16, 16], replicated, may hold values from 0 to 15, each once within a row
- conflict: int32 [16, 16], replicated, may hold values 0 or 1
Outputs:
- down_update: float32 [16, 32, 4608], P('task', None, 'shard')
- up_update: float32 [16, 32, 4608], P('task', None, 'shard')
The draws below stay inside these ranges and needn't reach their ends.
Inputs may be any that keep to these rules, and one draw needn't show every extreme that they name: `cotangent`: task gradients share common parts with task-dependent signs and sizes.
All inputs are finite; a program needn't handle non-finite values.
Results may differ from the reference program's by a relative error of at most 0.0004.
Values sent between devices are 32-bit elements; how exact they have to be, the bound alone decides.
No kernel may reach another device: no remote copies, remote signals or barrier semaphores. Data moves between devices by JAX's collectives and lax.ppermute only.
A program may use at most 64 MiB of HBM per device.

```python
import jax
import jax.numpy as jnp
from jax import lax

MODEL_WIDTH = 4608
EXPERT_COUNT = 16
EXPERT_RANK = 32
TASK_TOKENS = 512
NTASK = 16


def draw_cotangent(key, part):
    key = jax.random.fold_in(key, 7)
    key_common, key_own, key_mix = jax.random.split(key, 3)
    size = 0.5 * (EXPERT_COUNT / TASK_TOKENS) ** 0.5
    common_parts = 3
    common = jax.random.normal(key_common, (common_parts, TASK_TOKENS, MODEL_WIDTH), jnp.float32)
    own = 0.4 * jax.random.normal(key_own, (NTASK, TASK_TOKENS, MODEL_WIDTH), jnp.float32)
    rows = jnp.ones((1, TASK_TOKENS, 1), jnp.float32)
    mix = jax.random.uniform(key_mix, (NTASK, common_parts, 1, 1), jnp.float32, -1.0, 1.0)
    shared = jnp.sum(mix * common[None], axis=1)
    values = size * rows * (shared + own)
    return jnp.transpose(values, (0, 2, 1)).astype(jnp.bfloat16)


def plant(entries, stream_key, least, top_value):
    shape = entries.shape
    place = [jax.random.randint(jax.random.fold_in(stream_key, axis), (), 0, shape[axis]) for axis in range(len(shape))]
    entries = entries.at[tuple(place)].set(least)
    longest = shape.index(max(shape))
    place[longest] = (place[longest] + 1) % shape[longest]
    return entries.at[tuple(place)].set(top_value)


def block_levels(stream_key, dims, pieces, least, largest):
    gain, own = 1.0, jax.random.fold_in(stream_key, 6)
    for axis_at, shards_of in pieces:
        draws = jnp.exp(jax.random.uniform(jax.random.fold_in(own, axis_at), (shards_of,), jnp.float32, least / len(pieces), largest / len(pieces)))
        gain = gain * jnp.repeat(draws, dims[axis_at] // shards_of).reshape([-1 if axis == axis_at else 1 for axis in range(len(dims))])
    return gain


def normal_values(stream_key, shape, deviation, most, shards=(), kind=jnp.bfloat16):
    result = jax.random.normal(stream_key, shape, jnp.float32) * deviation
    if len(shards) > 0:
        result = block_levels(stream_key, shape, shards, -0.22, 0.18) * result
    return jnp.clip(result, min=-most, max=most).astype(kind)


def setup_inputs(seed: int = 0) -> dict:
    keys = jax.random.split(jax.random.key(seed), 8)
    return {
        "inputs": normal_values(keys[0], (MODEL_WIDTH, TASK_TOKENS), 1.0, 6.0, ((0, 32),)),
        "cotangent": draw_cotangent(jax.random.fold_in(keys[7], 71), 0),
        "routes": plant(jax.random.randint(keys[2], (NTASK, TASK_TOKENS), 0, EXPERT_COUNT), jax.random.fold_in(keys[2], 1), 0, EXPERT_COUNT - 1).astype(jnp.int32),
        "adapter_down_factor": normal_values(keys[3], (MODEL_WIDTH, EXPERT_COUNT * EXPERT_RANK), MODEL_WIDTH ** -0.5, 0.09375, ((0, 32),)),
        "adapter_up_factor": normal_values(keys[4], (MODEL_WIDTH, EXPERT_COUNT * EXPERT_RANK), MODEL_WIDTH ** -0.5, 0.09375, ((0, 32),)),
        "order": jax.vmap(lambda own: jax.random.permutation(own, NTASK))(jax.random.split(keys[5], NTASK)).reshape((NTASK, NTASK)).astype(jnp.int32),
        "conflict": plant((jax.random.randint(keys[6], (NTASK, NTASK), 0, 2) < 1).astype(jnp.int32), jax.random.fold_in(keys[6], 1), 0, 1),
    }


def per_task_gradient(cotangent_matrix, routing_row, inputs, adapter_down_factor, adapter_up_factor):
    across_model_width = (((0,), (0,)), ((), ()))
    encoded_full = lax.dot_general(inputs, adapter_down_factor, across_model_width, preferred_element_type=jnp.float32).reshape(TASK_TOKENS, EXPERT_COUNT, EXPERT_RANK)
    backward_full = lax.dot_general(cotangent_matrix, adapter_up_factor, across_model_width, preferred_element_type=jnp.float32).reshape(TASK_TOKENS, EXPERT_COUNT, EXPERT_RANK)
    onehot = (routing_row[:, None] == jnp.arange(EXPERT_COUNT, dtype=jnp.int32)[None, :]).astype(jnp.float32)
    code = 2.0 * jnp.sum(onehot[:, :, None] * encoded_full, axis=1)
    back = 2.0 * jnp.sum(onehot[:, :, None] * backward_full, axis=1)
    code_mask = (onehot[:, :, None] * code[:, None, :]).reshape(TASK_TOKENS, EXPERT_COUNT * EXPERT_RANK)
    back_mask = (onehot[:, :, None] * back[:, None, :]).reshape(TASK_TOKENS, EXPERT_COUNT * EXPERT_RANK)
    over_tokens = (((0,), (1,)), ((), ()))
    grad_down = lax.dot_general(back_mask, inputs.astype(jnp.float32), over_tokens, precision=lax.Precision.HIGHEST, preferred_element_type=jnp.float32)
    grad_up = lax.dot_general(code_mask, cotangent_matrix.astype(jnp.float32), over_tokens, precision=lax.Precision.HIGHEST, preferred_element_type=jnp.float32)
    return jnp.concatenate([grad_down.reshape(-1), grad_up.reshape(-1)])


def reference(inputs, cotangent, routes, adapter_down_factor, adapter_up_factor, order, conflict):
    gradient_list = []
    for task_number in range(NTASK):
        gradient_list.append(per_task_gradient(cotangent[task_number], routes[task_number], inputs, adapter_down_factor, adapter_up_factor))
    gradient_list = jnp.stack(gradient_list)
    norms = jnp.sum(gradient_list * gradient_list, axis=1)
    ident = jnp.eye(NTASK, dtype=jnp.float32)
    active = conflict.astype(jnp.float32) * (1.0 - ident)
    current = gradient_list
    for step in range(NTASK):
        picked = (order[:, step][:, None] == jnp.arange(NTASK, dtype=jnp.int32)[None, :]).astype(jnp.float32)
        partner = jnp.dot(picked, gradient_list, precision=lax.Precision.HIGHEST)
        inner = jnp.sum(current * partner, axis=1)
        factor = jnp.sum(active * picked, axis=1) * inner / (jnp.sum(norms[None, :] * picked, axis=1) + 1e-6)
        current = current - factor[:, None] * partner
    total = jnp.sum(current, axis=0)
    half = EXPERT_COUNT * EXPERT_RANK * MODEL_WIDTH
    return total[:half].reshape(EXPERT_COUNT, EXPERT_RANK, MODEL_WIDTH), total[half:].reshape(EXPERT_COUNT, EXPERT_RANK, MODEL_WIDTH)
```

```python
import functools

import jax
import jax.numpy as jnp
from jax import lax
from jax.experimental import pallas as pl
from jax.experimental.pallas import tpu as pltpu
from jax.sharding import PartitionSpec as P

EXPERTS = 16
RANK = 32
TOKENS = 512
TASKS = 16
SHARDS = 32
LOCAL = 144
LANES = 128
TAIL = LOCAL - LANES
ROWS = 2 * RANK + 8
VMEM = pl.BlockSpec(memory_space=pltpu.VMEM)
F32 = jnp.float32
BF16 = jnp.bfloat16


def call(kernel, out_shapes):
    return functools.partial(
        pl.pallas_call,
        kernel,
        out_shape=out_shapes,
        out_specs=jax.tree.map(lambda _: VMEM, out_shapes),
        compiler_params=pltpu.CompilerParams(vmem_limit_bytes=48 * 1024 * 1024),
    )


def over_features(factor, tokens):
    return lax.dot_general(
        factor, tokens, (((0,), (0,)), ((), ())), preferred_element_type=F32
    )


def encode_kernel(x_ref, c_ref, routes_ref, down_ref, up_ref, out_ref):
    route = routes_ref[...]
    for part, (tokens, factor) in enumerate(((x_ref, down_ref), (c_ref, up_ref))):
        full = over_features(factor[...], tokens[...])
        picked = jnp.zeros((RANK, TOKENS), F32)
        for e in range(EXPERTS):
            picked = picked + jnp.where(route == e, full[e * RANK : (e + 1) * RANK, :], 0.0)
        for i in range(4):
            for q in range(4):
                out_ref[part * 16 + i * 4 + q] = picked[8 * i : 8 * i + 8, q * LANES : (q + 1) * LANES]


def sum_kernel(y_ref, out_ref):
    total = y_ref[0]
    for s in range(1, y_ref.shape[0]):
        total = total + y_ref[s]
    out_ref[...] = jnp.broadcast_to(total[None], out_ref.shape)


def grad_kernel(y_ref, x_ref, c_ref, routes_ref, out_ref):
    route = routes_ref[...]
    pad = jnp.zeros((2 * LANES - LOCAL, TOKENS), BF16)
    for part, tokens in enumerate((c_ref, x_ref)):
        values = 2.0 * jnp.concatenate(
            [
                jnp.concatenate([y_ref[part * 16 + i * 4 + q] for q in range(4)], axis=1)
                for i in range(4)
            ],
            axis=0,
        )
        feats = jnp.concatenate([tokens[...], pad], axis=0)
        masked = jnp.concatenate(
            [jnp.where(route == e, values, 0.0) for e in range(EXPERTS)], axis=0
        )
        high = masked.astype(BF16)
        low = (masked - high.astype(F32)).astype(BF16)
        dims = (((1,), (1,)), ((), ()))
        grad = lax.dot_general(high, feats, dims, preferred_element_type=F32) + lax.dot_general(
            low, feats, dims, preferred_element_type=F32
        )
        first = RANK * (1 - part)
        for e in range(EXPERTS):
            out_ref[e, first : first + RANK, :] = grad[e * RANK : (e + 1) * RANK, :LANES]
            tail = jnp.zeros((8, LANES), F32)
            for i in range(4):
                piece = grad[e * RANK + 8 * i : e * RANK + 8 * i + 8, LANES:]
                slot = first // 8 + i
                tail = tail + (pltpu.roll(piece, slot * TAIL, 1) if slot else piece)
            if part == 0:
                out_ref[e, 2 * RANK :, :] = tail
            else:
                out_ref[e, 2 * RANK :, :] += tail


def gram_kernel(r_ref, out_ref, rows_ref):
    lane = lax.broadcasted_iota(jnp.int32, (TASKS, LANES), 1)
    for t in range(TASKS):
        mine = r_ref[t]
        for u in range(t, TASKS):
            rows_ref[t, u : u + 1] = jnp.sum(mine * r_ref[u], axis=0, keepdims=True)
            if u > t:
                rows_ref[u, t : t + 1] = rows_ref[t, u : u + 1]
    gram = jnp.zeros((TASKS, LANES), F32)
    for t in range(TASKS):
        gram = jnp.where(lane == t, jnp.sum(rows_ref[t], axis=1, keepdims=True), gram)
    packed = gram[:8] + pltpu.roll(gram[8:], TASKS, 1)
    out_ref[...] = jnp.broadcast_to(packed[None], out_ref.shape)


def lane_columns(square):
    wide = jnp.concatenate([square, jnp.zeros((TASKS, LANES - TASKS), F32)], axis=1)
    row = lax.broadcasted_iota(jnp.int32, (TASKS, LANES), 0)
    lane = lax.broadcasted_iota(jnp.int32, (TASKS, LANES), 1)
    out = jnp.zeros((TASKS, LANES), F32)
    for s in range(TASKS):
        line = jnp.sum(
            jnp.where(row == lane, jnp.broadcast_to(wide[:, s : s + 1], wide.shape), 0.0),
            axis=0,
            keepdims=True,
        )
        out = jnp.where(row == s, line, out)
    return out


def combine_kernel(g_ref, r_ref, order_ref, conflict_ref, down_ref, up_ref):
    row = lax.broadcasted_iota(jnp.int32, (TASKS, LANES), 0)
    lane = lax.broadcasted_iota(jnp.int32, (TASKS, LANES), 1)
    packed = g_ref[0]
    for t in range(1, TASKS):
        packed = packed + g_ref[t]
    gram = jnp.concatenate([packed, pltpu.roll(packed, LANES - TASKS, 1)], axis=0)
    ident = row == lane
    orders = lane_columns(order_ref[...].astype(F32))
    active = jnp.where(ident, 0.0, lane_columns(conflict_ref[...].astype(F32)))
    norms = jnp.sum(jnp.where(ident, gram, 0.0), axis=1, keepdims=True)
    columns = [jnp.broadcast_to(gram[:, j : j + 1], gram.shape) for j in range(TASKS)]
    rowf = row.astype(F32)
    coef = jnp.where(ident, 1.0, 0.0)
    for s in range(TASKS):
        pick = orders[s : s + 1, :]
        picked = jnp.where(rowf == pick, 1.0, 0.0)
        partner = jnp.zeros((TASKS, LANES), F32)
        for j in range(TASKS):
            partner = jnp.where(pick == float(j), columns[j], partner)
        scale = jnp.sum(active * picked, axis=0, keepdims=True) / (
            jnp.sum(norms * picked, axis=0, keepdims=True) + 1e-06
        )
        inner = jnp.sum(coef * partner, axis=0, keepdims=True)
        coef = coef - (scale * inner) * picked
    coef = jnp.where(lane < TASKS, coef, 0.0)
    weight = jnp.sum(coef, axis=1, keepdims=True)
    total = weight[0:1, :] * r_ref[0]
    for t in range(1, TASKS):
        total = total + weight[t : t + 1, :] * r_ref[t]
    tail = total[2 * RANK :, :]
    for part, out in enumerate((down_ref, up_ref)):
        out[0, :, :LANES] = total[part * RANK : (part + 1) * RANK, :]
        for i in range(4):
            slot = part * 4 + i
            piece = pltpu.roll(tail, LANES - slot * TAIL, 1) if slot else tail
            out[0, 8 * i : 8 * i + 8, LANES:] = piece[:, :TAIL]


def per_device(inputs, cotangent, routes, down_factor, up_factor, order, conflict):
    cot = cotangent[0]
    blocks = jax.ShapeDtypeStruct((SHARDS, 8, LANES), F32)
    gram_blocks = jax.ShapeDtypeStruct((TASKS, 8, LANES), F32)
    partial = call(encode_kernel, blocks)(in_specs=[VMEM] * 5)(inputs, cot, routes, down_factor, up_factor)
    pieces = lax.all_to_all(partial, "shard", 0, 0)
    mine = call(sum_kernel, blocks)(in_specs=[VMEM])(pieces)
    codes = lax.all_to_all(mine, "shard", 0, 0)
    grads = call(grad_kernel, jax.ShapeDtypeStruct((EXPERTS, ROWS, LANES), F32))(in_specs=[VMEM] * 4)(
        codes, inputs, cot, routes
    )
    owned = lax.all_to_all(grads, "task", 0, 0)
    gram = pl.pallas_call(
        gram_kernel,
        out_shape=blocks,
        in_specs=[VMEM],
        out_specs=VMEM,
        scratch_shapes=[pltpu.VMEM((TASKS, TASKS, LANES), F32)],
        compiler_params=pltpu.CompilerParams(vmem_limit_bytes=48 * 1024 * 1024),
    )(owned)
    gram = lax.all_to_all(gram, "shard", 0, 0)
    gram = call(sum_kernel, gram_blocks)(in_specs=[VMEM])(gram)
    gram = lax.all_to_all(gram, "task", 0, 0)
    out = jax.ShapeDtypeStruct((1, RANK, LOCAL), F32)
    down, up = call(combine_kernel, (out, out))(in_specs=[VMEM] * 4)(gram, owned, order, conflict)
    return down, up


def solution(mesh):
    placed = (
        P("shard", None),
        P("task", "shard", None),
        P("task", None),
        P("shard", None),
        P("shard", None),
        P(),
        P(),
    )
    return jax.shard_map(
        per_device,
        mesh=mesh,
        in_specs=placed,
        out_specs=(P("task", None, "shard"), P("task", None, "shard")),
        check_vma=False,
    )
```

```python
import functools

import jax
import jax.numpy as jnp
from jax import lax
from jax.experimental import pallas as pl
from jax.experimental.pallas import tpu as pltpu
from jax.sharding import PartitionSpec as P

EXPERTS = 16
RANK = 32
TOKENS = 512
TASKS = 16
SHARDS = 32
LOCAL = 144
LANES = 128
TAIL = LOCAL - LANES
ROWS = 2 * RANK + 8
VMEM = pl.BlockSpec(memory_space=pltpu.VMEM)
HBM = pl.BlockSpec(memory_space=pltpu.HBM)
F32 = jnp.float32
BF16 = jnp.bfloat16


def call(kernel, out_shapes):
    return functools.partial(
        pl.pallas_call,
        kernel,
        out_shape=out_shapes,
        out_specs=jax.tree.map(lambda _: VMEM, out_shapes),
        compiler_params=pltpu.CompilerParams(vmem_limit_bytes=48 * 1024 * 1024),
    )


def over_features(factor, tokens):
    return lax.dot_general(
        factor, tokens, (((0,), (0,)), ((), ())), preferred_element_type=F32
    )


def encode_kernel(x_hbm, c_hbm, routes_hbm, down_hbm, up_hbm, out_ref, x_ref, c_ref, routes_ref, down_ref, up_ref, sems):
    pairs = (
        (routes_hbm, routes_ref),
        (x_hbm, x_ref),
        (down_hbm, down_ref),
        (c_hbm, c_ref),
        (up_hbm, up_ref),
    )
    copies = [pltpu.make_async_copy(src, dst, sems.at[i]) for i, (src, dst) in enumerate(pairs)]
    for copy in copies:
        copy.start()
    copies[0].wait()
    route = routes_ref[...]
    for part, (tokens, factor) in enumerate(((x_ref, down_ref), (c_ref, up_ref))):
        copies[1 + 2 * part].wait()
        copies[2 + 2 * part].wait()
        full = over_features(factor[...], tokens[...])
        picked = jnp.zeros((RANK, TOKENS), F32)
        for e in range(EXPERTS):
            picked = picked + jnp.where(route == e, full[e * RANK : (e + 1) * RANK, :], 0.0)
        for i in range(4):
            for q in range(4):
                out_ref[part * 16 + i * 4 + q] = picked[8 * i : 8 * i + 8, q * LANES : (q + 1) * LANES]


def sum_kernel(y_ref, out_ref):
    total = y_ref[0]
    for s in range(1, y_ref.shape[0]):
        total = total + y_ref[s]
    out_ref[...] = jnp.broadcast_to(total[None], out_ref.shape)


def gram_sum_kernel(y_ref, out_ref):
    total = y_ref[0]
    for s in range(1, y_ref.shape[0]):
        total = total + y_ref[s]
    for half in range(2):
        line = total[4 * half : 4 * half + 1, :]
        for i in range(1, 4):
            line = line + pltpu.roll(total, 2 * TASKS * i, 1)[4 * half + i : 4 * half + i + 1, :]
        out_ref[:, half : half + 1, :] = jnp.broadcast_to(line[None], (TASKS, 1, LANES))


def grad_kernel(y_ref, x_ref, c_ref, routes_ref, out_ref):
    route = routes_ref[...]
    pad = jnp.zeros((2 * LANES - LOCAL, TOKENS), BF16)
    for part, tokens in enumerate((c_ref, x_ref)):
        values = 2.0 * jnp.concatenate(
            [
                jnp.concatenate([y_ref[part * 16 + i * 4 + q] for q in range(4)], axis=1)
                for i in range(4)
            ],
            axis=0,
        )
        feats = jnp.concatenate([tokens[...], pad], axis=0)
        masked = jnp.concatenate(
            [jnp.where(route == e, values, 0.0) for e in range(EXPERTS)], axis=0
        )
        high = masked.astype(BF16)
        low = (masked - high.astype(F32)).astype(BF16)
        dims = (((1,), (1,)), ((), ()))
        grad = lax.dot_general(high, feats, dims, preferred_element_type=F32) + lax.dot_general(
            low, feats, dims, preferred_element_type=F32
        )
        first = RANK * (1 - part)
        for e in range(EXPERTS):
            out_ref[e, first : first + RANK, :] = grad[e * RANK : (e + 1) * RANK, :LANES]
            tail = jnp.zeros((8, LANES), F32)
            for i in range(4):
                piece = grad[e * RANK + 8 * i : e * RANK + 8 * i + 8, LANES:]
                slot = first // 8 + i
                tail = tail + (pltpu.roll(piece, slot * TAIL, 1) if slot else piece)
            if part == 0:
                out_ref[e, 2 * RANK :, :] = tail
            else:
                out_ref[e, 2 * RANK :, :] += tail


def gram_kernel(r_ref, out_ref, rows_ref):
    lane = lax.broadcasted_iota(jnp.int32, (TASKS, LANES), 1)
    for t in range(TASKS):
        mine = r_ref[t]
        for u in range(t, TASKS):
            rows_ref[t, u : u + 1] = jnp.sum(mine * r_ref[u], axis=0, keepdims=True)
            if u > t:
                rows_ref[u, t : t + 1] = rows_ref[t, u : u + 1]
    gram = jnp.zeros((TASKS, LANES), F32)
    for t in range(TASKS):
        gram = jnp.where(lane == t, jnp.sum(rows_ref[t], axis=1, keepdims=True), gram)
    gram = jnp.where(lane < TASKS, gram, 0.0)
    packed = gram[:8] + pltpu.roll(gram[8:], TASKS, 1)
    out_ref[...] = jnp.broadcast_to(packed[None], out_ref.shape)


def lane_columns(square):
    wide = jnp.concatenate([square, jnp.zeros((TASKS, LANES - TASKS), F32)], axis=1)
    row = lax.broadcasted_iota(jnp.int32, (TASKS, LANES), 0)
    lane = lax.broadcasted_iota(jnp.int32, (TASKS, LANES), 1)
    out = jnp.zeros((TASKS, LANES), F32)
    for s in range(TASKS):
        line = jnp.sum(
            jnp.where(row == lane, jnp.broadcast_to(wide[:, s : s + 1], wide.shape), 0.0),
            axis=0,
            keepdims=True,
        )
        out = jnp.where(row == s, line, out)
    return out


def combine_kernel(g_ref, r_ref, order_ref, conflict_ref, down_ref, up_ref):
    row = lax.broadcasted_iota(jnp.int32, (TASKS, LANES), 0)
    lane = lax.broadcasted_iota(jnp.int32, (TASKS, LANES), 1)
    lines = g_ref[0]
    for t in range(1, TASKS):
        lines = lines + g_ref[t]
    packed = jnp.zeros((8, LANES), F32)
    for i in range(8):
        line = jnp.broadcast_to(lines[i // 4 : i // 4 + 1, :], (8, LANES))
        line = pltpu.roll(line, LANES - 2 * TASKS * (i % 4), 1) if i % 4 else line
        packed = jnp.where(row[:8] == i, line, packed)
    gram = jnp.concatenate([packed, pltpu.roll(packed, LANES - TASKS, 1)], axis=0)
    ident = row == lane
    orders = lane_columns(order_ref[...].astype(F32))
    active = jnp.where(ident, 0.0, lane_columns(conflict_ref[...].astype(F32)))
    norms = jnp.sum(jnp.where(ident, gram, 0.0), axis=1, keepdims=True)
    columns = [jnp.broadcast_to(gram[:, j : j + 1], gram.shape) for j in range(TASKS)]
    rowf = row.astype(F32)
    coef = jnp.where(ident, 1.0, 0.0)
    for s in range(TASKS):
        pick = orders[s : s + 1, :]
        picked = jnp.where(rowf == pick, 1.0, 0.0)
        partner = jnp.zeros((TASKS, LANES), F32)
        for j in range(TASKS):
            partner = jnp.where(pick == float(j), columns[j], partner)
        scale = jnp.sum(active * picked, axis=0, keepdims=True) / (
            jnp.sum(norms * picked, axis=0, keepdims=True) + 1e-06
        )
        inner = jnp.sum(coef * partner, axis=0, keepdims=True)
        coef = coef - (scale * inner) * picked
    coef = jnp.where(lane < TASKS, coef, 0.0)
    weight = jnp.sum(coef, axis=1, keepdims=True)
    total = weight[0:1, :] * r_ref[0]
    for t in range(1, TASKS):
        total = total + weight[t : t + 1, :] * r_ref[t]
    tail = total[2 * RANK :, :]
    for part, out in enumerate((down_ref, up_ref)):
        out[0, :, :LANES] = total[part * RANK : (part + 1) * RANK, :]
        for i in range(4):
            slot = part * 4 + i
            piece = pltpu.roll(tail, LANES - slot * TAIL, 1) if slot else tail
            out[0, 8 * i : 8 * i + 8, LANES:] = piece[:, :TAIL]


def per_device(inputs, cotangent, routes, down_factor, up_factor, order, conflict):
    cot = cotangent[0]
    blocks = jax.ShapeDtypeStruct((SHARDS, 8, LANES), F32)
    gram_blocks = jax.ShapeDtypeStruct((TASKS, 2, LANES), F32)
    partial = pl.pallas_call(
        encode_kernel,
        out_shape=blocks,
        in_specs=[HBM] * 5,
        out_specs=VMEM,
        scratch_shapes=[
            pltpu.VMEM((LOCAL, TOKENS), BF16),
            pltpu.VMEM((LOCAL, TOKENS), BF16),
            pltpu.VMEM((1, TOKENS), jnp.int32),
            pltpu.VMEM((LOCAL, TOKENS), BF16),
            pltpu.VMEM((LOCAL, TOKENS), BF16),
            pltpu.SemaphoreType.DMA((5,)),
        ],
        compiler_params=pltpu.CompilerParams(vmem_limit_bytes=48 * 1024 * 1024),
    )(*(pltpu.with_memory_space_constraint(a, pltpu.HBM) for a in (inputs, cot, routes, down_factor, up_factor)))
    pieces = lax.all_to_all(partial, "shard", 0, 0)
    mine = call(sum_kernel, blocks)(in_specs=[VMEM])(pieces)
    codes = lax.all_to_all(mine, "shard", 0, 0)
    grads = call(grad_kernel, jax.ShapeDtypeStruct((EXPERTS, ROWS, LANES), F32))(in_specs=[VMEM] * 4)(
        codes, inputs, cot, routes
    )
    owned = lax.all_to_all(grads, "task", 0, 0)
    gram = pl.pallas_call(
        gram_kernel,
        out_shape=blocks,
        in_specs=[VMEM],
        out_specs=VMEM,
        scratch_shapes=[pltpu.VMEM((TASKS, TASKS, LANES), F32)],
        compiler_params=pltpu.CompilerParams(vmem_limit_bytes=48 * 1024 * 1024),
    )(owned)
    gram = lax.all_to_all(gram, "shard", 0, 0)
    gram = call(gram_sum_kernel, gram_blocks)(in_specs=[VMEM])(gram)
    gram = lax.all_to_all(gram, "task", 0, 0)
    out = jax.ShapeDtypeStruct((1, RANK, LOCAL), F32)
    down, up = call(combine_kernel, (out, out))(in_specs=[VMEM] * 4)(gram, owned, order, conflict)
    return down, up


def solution(mesh):
    placed = (
        P("shard", None),
        P("task", "shard", None),
        P("task", None),
        P("shard", None),
        P("shard", None),
        P(),
        P(),
    )
    return jax.shard_map(
        per_device,
        mesh=mesh,
        in_specs=placed,
        out_specs=(P("task", None, "shard"), P("task", None, "shard")),
        check_vma=False,
    )
```

```python
import functools

import jax
import jax.numpy as jnp
from jax import lax
from jax.experimental import pallas as pl
from jax.experimental.pallas import tpu as pltpu
from jax.sharding import PartitionSpec as P

EXPERTS = 16
RANK = 32
TOKENS = 512
TASKS = 16
SHARDS = 32
LOCAL = 144
LANES = 128
TAIL = LOCAL - LANES
ROWS = 2 * RANK + 8
VMEM = pl.BlockSpec(memory_space=pltpu.VMEM)
HBM = pl.BlockSpec(memory_space=pltpu.HBM)
F32 = jnp.float32
BF16 = jnp.bfloat16


def call(kernel, out_shapes):
    return functools.partial(
        pl.pallas_call,
        kernel,
        out_shape=out_shapes,
        out_specs=jax.tree.map(lambda _: VMEM, out_shapes),
        compiler_params=pltpu.CompilerParams(vmem_limit_bytes=48 * 1024 * 1024),
    )


def over_features(factor, tokens):
    return lax.dot_general(
        factor, tokens, (((0,), (0,)), ((), ())), preferred_element_type=F32
    )


def lane_columns(square):
    row = lax.broadcasted_iota(jnp.int32, (TASKS, LANES), 0)
    lane = lax.broadcasted_iota(jnp.int32, (TASKS, LANES), 1)
    out = jnp.zeros((TASKS, LANES), square.dtype)
    for s in range(TASKS):
        column = jnp.broadcast_to(square[:, s : s + 1], out.shape)
        line = jnp.sum(jnp.where(row == lane, column, 0), axis=0, keepdims=True)
        out = jnp.where(row == s, line, out)
    return out


def encode_kernel(
    x_hbm,
    c_hbm,
    routes_hbm,
    down_hbm,
    up_hbm,
    order_hbm,
    conflict_hbm,
    out_ref,
    order_out,
    active_out,
    x_ref,
    c_ref,
    routes_ref,
    down_ref,
    up_ref,
    order_ref,
    conflict_ref,
    sems,
):
    pairs = (
        (routes_hbm, routes_ref),
        (x_hbm, x_ref),
        (down_hbm, down_ref),
        (c_hbm, c_ref),
        (up_hbm, up_ref),
        (order_hbm, order_ref),
        (conflict_hbm, conflict_ref),
    )
    copies = [pltpu.make_async_copy(src, dst, sems.at[i]) for i, (src, dst) in enumerate(pairs)]
    for copy in copies:
        copy.start()
    copies[5].wait()
    copies[6].wait()
    row = lax.broadcasted_iota(jnp.int32, (TASKS, LANES), 0)
    lane = lax.broadcasted_iota(jnp.int32, (TASKS, LANES), 1)
    orders = lane_columns(order_ref[...])
    conflicts = jnp.where(row == lane, 0, lane_columns(conflict_ref[...]))
    active = jnp.zeros((TASKS, LANES), jnp.int32)
    for j in range(TASKS):
        active = jnp.where(orders == j, conflicts[j : j + 1, :], active)
    order_out[...] = orders
    active_out[...] = jnp.where(lane < TASKS, active, 0).astype(F32)
    copies[0].wait()
    route = routes_ref[...]
    for part, (tokens, factor) in enumerate(((x_ref, down_ref), (c_ref, up_ref))):
        copies[1 + 2 * part].wait()
        copies[2 + 2 * part].wait()
        full = over_features(factor[...], tokens[...])
        picked = jnp.zeros((RANK, TOKENS), F32)
        for e in range(EXPERTS):
            picked = picked + jnp.where(route == e, full[e * RANK : (e + 1) * RANK, :], 0.0)
        for i in range(4):
            for q in range(4):
                out_ref[part * 16 + i * 4 + q] = picked[8 * i : 8 * i + 8, q * LANES : (q + 1) * LANES]


def sum_kernel(y_ref, out_ref):
    total = y_ref[0]
    for s in range(1, y_ref.shape[0]):
        total = total + y_ref[s]
    out_ref[...] = jnp.broadcast_to(total[None], out_ref.shape)


def gram_sum_kernel(y_ref, out_ref):
    total = y_ref[0]
    for s in range(1, y_ref.shape[0]):
        total = total + y_ref[s]
    for half in range(2):
        line = total[4 * half : 4 * half + 1, :]
        for i in range(1, 4):
            line = line + pltpu.roll(total, 2 * TASKS * i, 1)[4 * half + i : 4 * half + i + 1, :]
        out_ref[:, half : half + 1, :] = jnp.broadcast_to(line[None], (TASKS, 1, LANES))


def grad_kernel(y_ref, x_ref, c_ref, routes_ref, out_ref):
    route = routes_ref[...]
    pad = jnp.zeros((2 * LANES - LOCAL, TOKENS), BF16)
    for part, tokens in enumerate((c_ref, x_ref)):
        values = 2.0 * jnp.concatenate(
            [
                jnp.concatenate([y_ref[part * 16 + i * 4 + q] for q in range(4)], axis=1)
                for i in range(4)
            ],
            axis=0,
        )
        feats = jnp.concatenate([tokens[...], pad], axis=0)
        masked = jnp.concatenate(
            [jnp.where(route == e, values, 0.0) for e in range(EXPERTS)], axis=0
        )
        high = masked.astype(BF16)
        low = (masked - high.astype(F32)).astype(BF16)
        dims = (((1,), (1,)), ((), ()))
        grad = lax.dot_general(high, feats, dims, preferred_element_type=F32) + lax.dot_general(
            low, feats, dims, preferred_element_type=F32
        )
        first = RANK * (1 - part)
        for e in range(EXPERTS):
            out_ref[e, first : first + RANK, :] = grad[e * RANK : (e + 1) * RANK, :LANES]
            tail = jnp.zeros((8, LANES), F32)
            for i in range(4):
                piece = grad[e * RANK + 8 * i : e * RANK + 8 * i + 8, LANES:]
                slot = first // 8 + i
                tail = tail + (pltpu.roll(piece, slot * TAIL, 1) if slot else piece)
            if part == 0:
                out_ref[e, 2 * RANK :, :] = tail
            else:
                out_ref[e, 2 * RANK :, :] += tail


def gram_kernel(r_ref, out_ref, rows_ref):
    lane = lax.broadcasted_iota(jnp.int32, (TASKS, LANES), 1)
    for t in range(TASKS):
        mine = r_ref[t]
        for u in range(t, TASKS):
            rows_ref[t, u : u + 1] = jnp.sum(mine * r_ref[u], axis=0, keepdims=True)
            if u > t:
                rows_ref[u, t : t + 1] = rows_ref[t, u : u + 1]
    gram = jnp.zeros((TASKS, LANES), F32)
    for t in range(TASKS):
        gram = jnp.where(lane == t, jnp.sum(rows_ref[t], axis=1, keepdims=True), gram)
    gram = jnp.where(lane < TASKS, gram, 0.0)
    packed = gram[:8] + pltpu.roll(gram[8:], TASKS, 1)
    out_ref[...] = jnp.broadcast_to(packed[None], out_ref.shape)


def combine_kernel(g_ref, r_ref, order_ref, active_ref, down_ref, up_ref, partner_ref, scale_ref):
    row = lax.broadcasted_iota(jnp.int32, (TASKS, LANES), 0)
    lane = lax.broadcasted_iota(jnp.int32, (TASKS, LANES), 1)
    lines = g_ref[0]
    for t in range(1, TASKS):
        lines = lines + g_ref[t]
    packed = jnp.zeros((8, LANES), F32)
    for i in range(8):
        line = jnp.broadcast_to(lines[i // 4 : i // 4 + 1, :], (8, LANES))
        line = pltpu.roll(line, LANES - 2 * TASKS * (i % 4), 1) if i % 4 else line
        packed = jnp.where(row[:8] == i, line, packed)
    gram = jnp.concatenate([packed, pltpu.roll(packed, LANES - TASKS, 1)], axis=0)
    orders = order_ref[...]
    norm = jnp.sum(jnp.where(row == lane, gram, 0.0), axis=0, keepdims=True)
    norm = jnp.take_along_axis(jnp.broadcast_to(norm, gram.shape), orders, axis=1)
    scale_ref[...] = active_ref[...] / (norm + 1e-06)
    for k in range(TASKS):
        line = jnp.broadcast_to(gram[k : k + 1, :], gram.shape)
        partner_ref[k] = jnp.take_along_axis(line, orders, axis=1)
    full = (8, LANES)
    coef = [jnp.where(lane[:8] == k, 1.0, 0.0) for k in range(TASKS)]
    for s in range(TASKS):
        terms = [coef[k] * jnp.broadcast_to(partner_ref[k, s : s + 1, :], full) for k in range(TASKS)]
        while len(terms) > 1:
            terms = [a + b for a, b in zip(terms[::2], terms[1::2])]
        factor = jnp.broadcast_to(scale_ref[s : s + 1, :], full) * terms[0]
        pick = jnp.broadcast_to(order_ref[s : s + 1, :], full)
        coef = [coef[k] - jnp.where(pick == k, factor, 0.0) for k in range(TASKS)]
    total = None
    for t in range(TASKS):
        weight = jnp.sum(coef[t], axis=1, keepdims=True)[:1]
        term = weight * r_ref[t]
        total = term if total is None else total + term
    tail = total[2 * RANK :, :]
    for part, out in enumerate((down_ref, up_ref)):
        out[0, :, :LANES] = total[part * RANK : (part + 1) * RANK, :]
        for i in range(4):
            slot = part * 4 + i
            piece = pltpu.roll(tail, LANES - slot * TAIL, 1) if slot else tail
            out[0, 8 * i : 8 * i + 8, LANES:] = piece[:, :TAIL]


def per_device(inputs, cotangent, routes, down_factor, up_factor, order, conflict):
    cot = cotangent[0]
    blocks = jax.ShapeDtypeStruct((SHARDS, 8, LANES), F32)
    gram_blocks = jax.ShapeDtypeStruct((TASKS, 2, LANES), F32)
    plan = (
        jax.ShapeDtypeStruct((TASKS, LANES), jnp.int32),
        jax.ShapeDtypeStruct((TASKS, LANES), F32),
    )
    partial, orders, active = pl.pallas_call(
        encode_kernel,
        out_shape=(blocks, *plan),
        in_specs=[HBM] * 7,
        out_specs=(VMEM,) * 3,
        scratch_shapes=[
            pltpu.VMEM((LOCAL, TOKENS), BF16),
            pltpu.VMEM((LOCAL, TOKENS), BF16),
            pltpu.VMEM((1, TOKENS), jnp.int32),
            pltpu.VMEM((LOCAL, TOKENS), BF16),
            pltpu.VMEM((LOCAL, TOKENS), BF16),
            pltpu.VMEM((TASKS, TASKS), jnp.int32),
            pltpu.VMEM((TASKS, TASKS), jnp.int32),
            pltpu.SemaphoreType.DMA((7,)),
        ],
        compiler_params=pltpu.CompilerParams(vmem_limit_bytes=48 * 1024 * 1024),
    )(*(pltpu.with_memory_space_constraint(a, pltpu.HBM) for a in (inputs, cot, routes, down_factor, up_factor, order, conflict)))
    pieces = lax.all_to_all(partial, "shard", 0, 0)
    mine = call(sum_kernel, blocks)(in_specs=[VMEM])(pieces)
    codes = lax.all_to_all(mine, "shard", 0, 0)
    grads = call(grad_kernel, jax.ShapeDtypeStruct((EXPERTS, ROWS, LANES), F32))(in_specs=[VMEM] * 4)(
        codes, inputs, cot, routes
    )
    owned = lax.all_to_all(grads, "task", 0, 0)
    gram = pl.pallas_call(
        gram_kernel,
        out_shape=blocks,
        in_specs=[VMEM],
        out_specs=VMEM,
        scratch_shapes=[pltpu.VMEM((TASKS, TASKS, LANES), F32)],
        compiler_params=pltpu.CompilerParams(vmem_limit_bytes=48 * 1024 * 1024),
    )(owned)
    gram = lax.all_to_all(gram, "shard", 0, 0)
    gram = call(gram_sum_kernel, gram_blocks)(in_specs=[VMEM])(gram)
    gram = lax.all_to_all(gram, "task", 0, 0)
    out = jax.ShapeDtypeStruct((1, RANK, LOCAL), F32)
    return pl.pallas_call(
        combine_kernel,
        out_shape=(out, out),
        in_specs=[VMEM] * 4,
        out_specs=(VMEM, VMEM),
        scratch_shapes=[pltpu.VMEM((TASKS, TASKS, LANES), F32), pltpu.VMEM((TASKS, LANES), F32)],
        compiler_params=pltpu.CompilerParams(vmem_limit_bytes=48 * 1024 * 1024),
    )(gram, owned, orders, active)


def solution(mesh):
    placed = (
        P("shard", None),
        P("task", "shard", None),
        P("task", None),
        P("shard", None),
        P("shard", None),
        P(),
        P(),
    )
    return jax.shard_map(
        per_device,
        mesh=mesh,
        in_specs=placed,
        out_specs=(P("task", None, "shard"), P("task", None, "shard")),
        check_vma=False,
    )
```

```python
import functools

import jax
import jax.numpy as jnp
from jax import lax
from jax.experimental import pallas as pl
from jax.experimental.pallas import tpu as pltpu
from jax.sharding import PartitionSpec as P

EXPERTS = 16
RANK = 32
TOKENS = 512
TASKS = 16
SHARDS = 32
LOCAL = 144
LANES = 128
TAIL = LOCAL - LANES
TILES = 2 * RANK // 8 + 1
VMEM = pl.BlockSpec(memory_space=pltpu.VMEM)
HBM = pl.BlockSpec(memory_space=pltpu.HBM)
F32 = jnp.float32
BF16 = jnp.bfloat16


def call(kernel, out_shapes):
    return functools.partial(
        pl.pallas_call,
        kernel,
        out_shape=out_shapes,
        out_specs=jax.tree.map(lambda _: VMEM, out_shapes),
        compiler_params=pltpu.CompilerParams(vmem_limit_bytes=48 * 1024 * 1024),
    )


def over_features(factor, tokens):
    return lax.dot_general(
        factor, tokens, (((0,), (0,)), ((), ())), preferred_element_type=F32
    )


def lane_columns(square):
    row = lax.broadcasted_iota(jnp.int32, (TASKS, LANES), 0)
    lane = lax.broadcasted_iota(jnp.int32, (TASKS, LANES), 1)
    out = jnp.zeros((TASKS, LANES), square.dtype)
    for s in range(TASKS):
        column = jnp.broadcast_to(square[:, s : s + 1], out.shape)
        line = jnp.sum(jnp.where(row == lane, column, 0), axis=0, keepdims=True)
        out = jnp.where(row == s, line, out)
    return out


def encode_kernel(
    x_hbm,
    c_hbm,
    routes_hbm,
    down_hbm,
    up_hbm,
    order_hbm,
    conflict_hbm,
    out_ref,
    order_out,
    active_out,
    x_ref,
    c_ref,
    routes_ref,
    down_ref,
    up_ref,
    order_ref,
    conflict_ref,
    sems,
):
    pairs = (
        (routes_hbm, routes_ref),
        (x_hbm, x_ref),
        (down_hbm, down_ref),
        (c_hbm, c_ref),
        (up_hbm, up_ref),
        (order_hbm, order_ref),
        (conflict_hbm, conflict_ref),
    )
    copies = [pltpu.make_async_copy(src, dst, sems.at[i]) for i, (src, dst) in enumerate(pairs)]
    for copy in copies:
        copy.start()
    copies[5].wait()
    copies[6].wait()
    row = lax.broadcasted_iota(jnp.int32, (TASKS, LANES), 0)
    lane = lax.broadcasted_iota(jnp.int32, (TASKS, LANES), 1)
    orders = lane_columns(order_ref[...])
    conflicts = jnp.where(row == lane, 0, lane_columns(conflict_ref[...]))
    active = jnp.zeros((TASKS, LANES), jnp.int32)
    for j in range(TASKS):
        active = jnp.where(orders == j, conflicts[j : j + 1, :], active)
    order_out[...] = orders
    active_out[...] = jnp.where(lane < TASKS, active, 0).astype(F32)
    copies[0].wait()
    route = routes_ref[...]
    for part, (tokens, factor) in enumerate(((x_ref, down_ref), (c_ref, up_ref))):
        copies[1 + 2 * part].wait()
        copies[2 + 2 * part].wait()
        full = over_features(factor[...], tokens[...])
        picked = jnp.zeros((RANK, TOKENS), F32)
        for e in range(EXPERTS):
            picked = picked + jnp.where(route == e, full[e * RANK : (e + 1) * RANK, :], 0.0)
        for i in range(4):
            for q in range(4):
                out_ref[part * 16 + i * 4 + q] = picked[8 * i : 8 * i + 8, q * LANES : (q + 1) * LANES]


def sum_kernel(y_ref, out_ref):
    total = y_ref[0]
    for s in range(1, y_ref.shape[0]):
        total = total + y_ref[s]
    out_ref[...] = jnp.broadcast_to(total[None], out_ref.shape)


def gram_sum_kernel(y_ref, out_ref):
    total = y_ref[0]
    for s in range(1, y_ref.shape[0]):
        total = total + y_ref[s]
    for half in range(2):
        line = total[4 * half : 4 * half + 1, :]
        for i in range(1, 4):
            line = line + pltpu.roll(total, 2 * TASKS * i, 1)[4 * half + i : 4 * half + i + 1, :]
        out_ref[:, half : half + 1, :] = jnp.broadcast_to(line[None], (TASKS, 1, LANES))


def grad_kernel(y_ref, x_ref, c_ref, routes_ref, out_ref):
    route = routes_ref[...]
    pad = jnp.zeros((2 * LANES - LOCAL, TOKENS), BF16)
    for part, tokens in enumerate((c_ref, x_ref)):
        values = 2.0 * jnp.concatenate(
            [
                jnp.concatenate([y_ref[part * 16 + i * 4 + q] for q in range(4)], axis=1)
                for i in range(4)
            ],
            axis=0,
        )
        feats = jnp.concatenate([tokens[...], pad], axis=0)
        masked = jnp.concatenate(
            [jnp.where(route == e, values, 0.0) for e in range(EXPERTS)], axis=0
        )
        high = masked.astype(BF16)
        low = (masked - high.astype(F32)).astype(BF16)
        dims = (((1,), (1,)), ((), ()))
        grad = lax.dot_general(high, feats, dims, preferred_element_type=F32) + lax.dot_general(
            low, feats, dims, preferred_element_type=F32
        )
        first = RANK * (1 - part)
        for e in range(EXPERTS):
            tail = jnp.zeros((8, LANES), F32)
            for i in range(4):
                slot = first // 8 + i
                rows = slice(e * RANK + 8 * i, e * RANK + 8 * i + 8)
                out_ref[e, :, slot * LANES : (slot + 1) * LANES] = grad[rows, :LANES]
                piece = grad[rows, LANES:]
                tail = tail + (pltpu.roll(piece, slot * TAIL, 1) if slot else piece)
            if part == 0:
                out_ref[e, :, (TILES - 1) * LANES :] = tail
            else:
                out_ref[e, :, (TILES - 1) * LANES :] += tail


def gram_kernel(r_ref, out_ref, rows_ref):
    lane = lax.broadcasted_iota(jnp.int32, (TASKS, LANES), 1)
    for t in range(TASKS):
        mine = [r_ref[t, :, k * LANES : (k + 1) * LANES] for k in range(TILES)]
        for u in range(t, TASKS):
            dot = mine[0] * r_ref[u, :, :LANES]
            for k in range(1, TILES):
                dot = dot + mine[k] * r_ref[u, :, k * LANES : (k + 1) * LANES]
            rows_ref[t, u : u + 1] = jnp.sum(dot, axis=0, keepdims=True)
            if u > t:
                rows_ref[u, t : t + 1] = rows_ref[t, u : u + 1]
    gram = jnp.zeros((TASKS, LANES), F32)
    for t in range(TASKS):
        gram = jnp.where(lane == t, jnp.sum(rows_ref[t], axis=1, keepdims=True), gram)
    gram = jnp.where(lane < TASKS, gram, 0.0)
    packed = gram[:8] + pltpu.roll(gram[8:], TASKS, 1)
    out_ref[...] = jnp.broadcast_to(packed[None], out_ref.shape)


def combine_kernel(g_ref, r_ref, order_ref, active_ref, down_ref, up_ref, partner_ref, scale_ref):
    row = lax.broadcasted_iota(jnp.int32, (TASKS, LANES), 0)
    lane = lax.broadcasted_iota(jnp.int32, (TASKS, LANES), 1)
    lines = g_ref[0]
    for t in range(1, TASKS):
        lines = lines + g_ref[t]
    packed = jnp.zeros((8, LANES), F32)
    for i in range(8):
        line = jnp.broadcast_to(lines[i // 4 : i // 4 + 1, :], (8, LANES))
        line = pltpu.roll(line, LANES - 2 * TASKS * (i % 4), 1) if i % 4 else line
        packed = jnp.where(row[:8] == i, line, packed)
    gram = jnp.concatenate([packed, pltpu.roll(packed, LANES - TASKS, 1)], axis=0)
    orders = order_ref[...]
    norm = jnp.sum(jnp.where(row == lane, gram, 0.0), axis=0, keepdims=True)
    norm = jnp.take_along_axis(jnp.broadcast_to(norm, gram.shape), orders, axis=1)
    scale_ref[...] = active_ref[...] / (norm + 1e-06)
    for k in range(TASKS):
        line = jnp.broadcast_to(gram[k : k + 1, :], gram.shape)
        partner_ref[k] = jnp.take_along_axis(line, orders, axis=1)
    full = (8, LANES)
    coef = [jnp.where(lane[:8] == k, 1.0, 0.0) for k in range(TASKS)]
    for s in range(TASKS):
        terms = [coef[k] * jnp.broadcast_to(partner_ref[k, s : s + 1, :], full) for k in range(TASKS)]
        while len(terms) > 1:
            terms = [a + b for a, b in zip(terms[::2], terms[1::2])]
        factor = jnp.broadcast_to(scale_ref[s : s + 1, :], full) * terms[0]
        pick = jnp.broadcast_to(order_ref[s : s + 1, :], full)
        coef = [coef[k] - jnp.where(pick == k, factor, 0.0) for k in range(TASKS)]
    total = None
    for t in range(TASKS):
        weight = jnp.sum(coef[t], axis=1, keepdims=True)[:1]
        term = weight * r_ref[t]
        total = term if total is None else total + term
    tail = total[:, (TILES - 1) * LANES :]
    for part, out in enumerate((down_ref, up_ref)):
        for i in range(4):
            slot = part * 4 + i
            out[0, 8 * i : 8 * i + 8, :LANES] = total[:, slot * LANES : (slot + 1) * LANES]
            piece = pltpu.roll(tail, LANES - slot * TAIL, 1) if slot else tail
            out[0, 8 * i : 8 * i + 8, LANES:] = piece[:, :TAIL]


def per_device(inputs, cotangent, routes, down_factor, up_factor, order, conflict):
    cot = cotangent[0]
    blocks = jax.ShapeDtypeStruct((SHARDS, 8, LANES), F32)
    gram_blocks = jax.ShapeDtypeStruct((TASKS, 2, LANES), F32)
    plan = (
        jax.ShapeDtypeStruct((TASKS, LANES), jnp.int32),
        jax.ShapeDtypeStruct((TASKS, LANES), F32),
    )
    partial, orders, active = pl.pallas_call(
        encode_kernel,
        out_shape=(blocks, *plan),
        in_specs=[HBM] * 7,
        out_specs=(VMEM,) * 3,
        scratch_shapes=[
            pltpu.VMEM((LOCAL, TOKENS), BF16),
            pltpu.VMEM((LOCAL, TOKENS), BF16),
            pltpu.VMEM((1, TOKENS), jnp.int32),
            pltpu.VMEM((LOCAL, TOKENS), BF16),
            pltpu.VMEM((LOCAL, TOKENS), BF16),
            pltpu.VMEM((TASKS, TASKS), jnp.int32),
            pltpu.VMEM((TASKS, TASKS), jnp.int32),
            pltpu.SemaphoreType.DMA((7,)),
        ],
        compiler_params=pltpu.CompilerParams(vmem_limit_bytes=48 * 1024 * 1024),
    )(*(pltpu.with_memory_space_constraint(a, pltpu.HBM) for a in (inputs, cot, routes, down_factor, up_factor, order, conflict)))
    pieces = lax.all_to_all(partial, "shard", 0, 0)
    mine = call(sum_kernel, blocks)(in_specs=[VMEM])(pieces)
    codes = lax.all_to_all(mine, "shard", 0, 0)
    grads = call(grad_kernel, jax.ShapeDtypeStruct((EXPERTS, 8, TILES * LANES), F32))(in_specs=[VMEM] * 4)(
        codes, inputs, cot, routes
    )
    owned = lax.all_to_all(grads, "task", 0, 0)
    gram = pl.pallas_call(
        gram_kernel,
        out_shape=blocks,
        in_specs=[VMEM],
        out_specs=VMEM,
        scratch_shapes=[pltpu.VMEM((TASKS, TASKS, LANES), F32)],
        compiler_params=pltpu.CompilerParams(vmem_limit_bytes=48 * 1024 * 1024),
    )(owned)
    gram = lax.all_to_all(gram, "shard", 0, 0)
    gram = call(gram_sum_kernel, gram_blocks)(in_specs=[VMEM])(gram)
    gram = lax.all_to_all(gram, "task", 0, 0)
    out = jax.ShapeDtypeStruct((1, RANK, LOCAL), F32)
    return pl.pallas_call(
        combine_kernel,
        out_shape=(out, out),
        in_specs=[VMEM] * 4,
        out_specs=(VMEM, VMEM),
        scratch_shapes=[pltpu.VMEM((TASKS, TASKS, LANES), F32), pltpu.VMEM((TASKS, LANES), F32)],
        compiler_params=pltpu.CompilerParams(vmem_limit_bytes=48 * 1024 * 1024),
    )(gram, owned, orders, active)


def solution(mesh):
    placed = (
        P("shard", None),
        P("task", "shard", None),
        P("task", None),
        P("shard", None),
        P("shard", None),
        P(),
        P(),
    )
    return jax.shard_map(
        per_device,
        mesh=mesh,
        in_specs=placed,
        out_specs=(P("task", None, "shard"), P("task", None, "shard")),
        check_vma=False,
    )
```

```python
import functools

import jax
import jax.numpy as jnp
from jax import lax
from jax.experimental import pallas as pl
from jax.experimental.pallas import tpu as pltpu
from jax.sharding import PartitionSpec as P

EXPERTS = 16
RANK = 32
TOKENS = 512
TASKS = 16
SHARDS = 32
LOCAL = 144
LANES = 128
TAIL = LOCAL - LANES
TILES = 2 * RANK // 8 + 1
VMEM = pl.BlockSpec(memory_space=pltpu.VMEM)
HBM = pl.BlockSpec(memory_space=pltpu.HBM)
F32 = jnp.float32
BF16 = jnp.bfloat16


def call(kernel, out_shapes):
    return functools.partial(
        pl.pallas_call,
        kernel,
        out_shape=out_shapes,
        out_specs=jax.tree.map(lambda _: VMEM, out_shapes),
        compiler_params=pltpu.CompilerParams(vmem_limit_bytes=48 * 1024 * 1024),
    )


def over_features(factor, tokens):
    return lax.dot_general(
        factor, tokens, (((0,), (0,)), ((), ())), preferred_element_type=F32
    )


def lane_columns(square):
    row = lax.broadcasted_iota(jnp.int32, (TASKS, LANES), 0)
    lane = lax.broadcasted_iota(jnp.int32, (TASKS, LANES), 1)
    out = jnp.zeros((TASKS, LANES), square.dtype)
    for s in range(TASKS):
        column = jnp.broadcast_to(square[:, s : s + 1], out.shape)
        line = jnp.sum(jnp.where(row == lane, column, 0), axis=0, keepdims=True)
        out = jnp.where(row == s, line, out)
    return out


def encode_kernel(
    x_hbm,
    c_hbm,
    routes_hbm,
    down_hbm,
    up_hbm,
    order_hbm,
    conflict_hbm,
    out_ref,
    order_out,
    active_out,
    x_ref,
    c_ref,
    routes_ref,
    down_ref,
    up_ref,
    order_ref,
    conflict_ref,
    sems,
):
    pairs = (
        (routes_hbm, routes_ref),
        (x_hbm, x_ref),
        (down_hbm, down_ref),
        (c_hbm, c_ref),
        (up_hbm, up_ref),
        (order_hbm, order_ref),
        (conflict_hbm, conflict_ref),
    )
    copies = [pltpu.make_async_copy(src, dst, sems.at[i]) for i, (src, dst) in enumerate(pairs)]
    for copy in copies:
        copy.start()
    copies[5].wait()
    copies[6].wait()
    row = lax.broadcasted_iota(jnp.int32, (TASKS, LANES), 0)
    lane = lax.broadcasted_iota(jnp.int32, (TASKS, LANES), 1)
    orders = lane_columns(order_ref[...])
    conflicts = jnp.where(row == lane, 0, lane_columns(conflict_ref[...]))
    active = jnp.zeros((TASKS, LANES), jnp.int32)
    for j in range(TASKS):
        active = jnp.where(orders == j, conflicts[j : j + 1, :], active)
    order_out[...] = orders
    active_out[...] = jnp.where(lane < TASKS, active, 0).astype(F32)
    copies[0].wait()
    route = routes_ref[...]
    for part, (tokens, factor) in enumerate(((x_ref, down_ref), (c_ref, up_ref))):
        copies[1 + 2 * part].wait()
        copies[2 + 2 * part].wait()
        full = over_features(factor[...], tokens[...])
        picked = jnp.zeros((RANK, TOKENS), F32)
        for e in range(EXPERTS):
            picked = picked + jnp.where(route == e, full[e * RANK : (e + 1) * RANK, :], 0.0)
        for i in range(4):
            for q in range(4):
                out_ref[part * 16 + i * 4 + q] = picked[8 * i : 8 * i + 8, q * LANES : (q + 1) * LANES]


def sum_kernel(y_ref, out_ref):
    total = y_ref[0]
    for s in range(1, y_ref.shape[0]):
        total = total + y_ref[s]
    out_ref[...] = jnp.broadcast_to(total[None], out_ref.shape)


def grad_kernel(y_ref, x_ref, c_ref, routes_ref, out_ref):
    route = jnp.broadcast_to(routes_ref[...], (RANK, TOKENS))
    onehot = [jnp.where(route == e, 1.0, 0.0).astype(BF16) for e in range(EXPERTS)]
    pad = jnp.zeros((2 * LANES - LOCAL, TOKENS), BF16)
    for part, tokens in enumerate((c_ref, x_ref)):
        values = 2.0 * jnp.concatenate(
            [
                jnp.concatenate([y_ref[part * 16 + i * 4 + q] for q in range(4)], axis=1)
                for i in range(4)
            ],
            axis=0,
        )
        feats = jnp.concatenate([tokens[...], pad], axis=0)
        high = values.astype(BF16)
        low = (values - high.astype(F32)).astype(BF16)
        high = jnp.concatenate([high * hot for hot in onehot], axis=0)
        low = jnp.concatenate([low * hot for hot in onehot], axis=0)
        dims = (((1,), (1,)), ((), ()))
        grad = lax.dot_general(high, feats, dims, preferred_element_type=F32) + lax.dot_general(
            low, feats, dims, preferred_element_type=F32
        )
        first = RANK * (1 - part)
        for e in range(EXPERTS):
            tail = jnp.zeros((8, LANES), F32)
            for i in range(4):
                slot = first // 8 + i
                rows = slice(e * RANK + 8 * i, e * RANK + 8 * i + 8)
                out_ref[e, :, slot * LANES : (slot + 1) * LANES] = grad[rows, :LANES]
                piece = grad[rows, LANES:]
                tail = tail + (pltpu.roll(piece, slot * TAIL, 1) if slot else piece)
            if part == 0:
                out_ref[e, :, (TILES - 1) * LANES :] = tail
            else:
                out_ref[e, :, (TILES - 1) * LANES :] += tail


def gram_row(t, u):
    at = t // 8 * LANES + (7 - t % 8) * TASKS + u
    return slice(at, at + 1)


def gram_kernel(r_ref, out_ref, rows_ref):
    for t in range(TASKS):
        mine = [r_ref[t, :, k * LANES : (k + 1) * LANES] for k in range(TILES)]
        for u in range(t, TASKS):
            dot = mine[0] * r_ref[u, :, :LANES]
            for k in range(1, TILES):
                dot = dot + mine[k] * r_ref[u, :, k * LANES : (k + 1) * LANES]
            dot = jnp.sum(dot, axis=0, keepdims=True)
            rows_ref[gram_row(t, u)] = dot
            if u > t:
                rows_ref[gram_row(u, t)] = dot
    rest = rows_ref[...]
    lines = jnp.zeros((8, 2 * LANES), F32)
    for _ in range(3):
        piece = rest.astype(BF16)
        rest = rest - piece.astype(F32)
        lines = lines + lax.dot_general(
            jnp.ones((8, LANES), BF16), piece, (((1,), (1,)), ((), ())), preferred_element_type=F32
        )
    for half in range(2):
        line = lines[:1, half * LANES : (half + 1) * LANES]
        out_ref[:, half : half + 1, :] = jnp.broadcast_to(line[None], (SHARDS, 1, LANES))


def combine_kernel(g_ref, r_ref, order_ref, active_ref, down_ref, up_ref, partner_ref, scale_ref):
    row = lax.broadcasted_iota(jnp.int32, (TASKS, LANES), 0)
    lane = lax.broadcasted_iota(jnp.int32, (TASKS, LANES), 1)
    lines = g_ref[0]
    for t in range(1, TASKS):
        lines = lines + g_ref[t]
    gram = jnp.concatenate(
        [
            pltpu.roll(
                jnp.broadcast_to(lines[i : i + 1, :], (8, LANES)), TASKS, 1, stride=TASKS, stride_axis=0
            )
            for i in range(2)
        ],
        axis=0,
    )
    orders = order_ref[...]
    norm = jnp.sum(jnp.where(row == lane, gram, 0.0), axis=0, keepdims=True)
    norm = jnp.take_along_axis(jnp.broadcast_to(norm, gram.shape), orders, axis=1)
    scale_ref[...] = active_ref[...] / (norm + 1e-06)
    for k in range(TASKS):
        line = jnp.broadcast_to(gram[k : k + 1, :], gram.shape)
        partner_ref[k] = jnp.take_along_axis(line, orders, axis=1)
    full = (8, LANES)
    coef = [jnp.where(lane[:8] == k, 1.0, 0.0) for k in range(TASKS)]
    for s in range(TASKS):
        terms = [coef[k] * jnp.broadcast_to(partner_ref[k, s : s + 1, :], full) for k in range(TASKS)]
        while len(terms) > 1:
            terms = [a + b for a, b in zip(terms[::2], terms[1::2])]
        factor = jnp.broadcast_to(scale_ref[s : s + 1, :], full) * terms[0]
        pick = jnp.broadcast_to(order_ref[s : s + 1, :], full)
        coef = [coef[k] - jnp.where(pick == k, factor, 0.0) for k in range(TASKS)]
    total = None
    for t in range(TASKS):
        weight = jnp.sum(coef[t], axis=1, keepdims=True)[:1]
        term = weight * r_ref[t]
        total = term if total is None else total + term
    tail = total[:, (TILES - 1) * LANES :]
    for part, out in enumerate((down_ref, up_ref)):
        for i in range(4):
            slot = part * 4 + i
            out[0, 8 * i : 8 * i + 8, :LANES] = total[:, slot * LANES : (slot + 1) * LANES]
            piece = pltpu.roll(tail, LANES - slot * TAIL, 1) if slot else tail
            out[0, 8 * i : 8 * i + 8, LANES:] = piece[:, :TAIL]


def per_device(inputs, cotangent, routes, down_factor, up_factor, order, conflict):
    cot = cotangent[0]
    blocks = jax.ShapeDtypeStruct((SHARDS, 8, LANES), F32)
    gram_blocks = jax.ShapeDtypeStruct((TASKS, 2, LANES), F32)
    plan = (
        jax.ShapeDtypeStruct((TASKS, LANES), jnp.int32),
        jax.ShapeDtypeStruct((TASKS, LANES), F32),
    )
    partial, orders, active = pl.pallas_call(
        encode_kernel,
        out_shape=(blocks, *plan),
        in_specs=[HBM] * 7,
        out_specs=(VMEM,) * 3,
        scratch_shapes=[
            pltpu.VMEM((LOCAL, TOKENS), BF16),
            pltpu.VMEM((LOCAL, TOKENS), BF16),
            pltpu.VMEM((1, TOKENS), jnp.int32),
            pltpu.VMEM((LOCAL, TOKENS), BF16),
            pltpu.VMEM((LOCAL, TOKENS), BF16),
            pltpu.VMEM((TASKS, TASKS), jnp.int32),
            pltpu.VMEM((TASKS, TASKS), jnp.int32),
            pltpu.SemaphoreType.DMA((7,)),
        ],
        compiler_params=pltpu.CompilerParams(vmem_limit_bytes=48 * 1024 * 1024),
    )(*(pltpu.with_memory_space_constraint(a, pltpu.HBM) for a in (inputs, cot, routes, down_factor, up_factor, order, conflict)))
    pieces = lax.all_to_all(partial, "shard", 0, 0)
    mine = call(sum_kernel, blocks)(in_specs=[VMEM])(pieces)
    codes = lax.all_to_all(mine, "shard", 0, 0)
    grads = call(grad_kernel, jax.ShapeDtypeStruct((EXPERTS, 8, TILES * LANES), F32))(in_specs=[VMEM] * 4)(
        codes, inputs, cot, routes
    )
    owned = lax.all_to_all(grads, "task", 0, 0)
    gram = pl.pallas_call(
        gram_kernel,
        out_shape=jax.ShapeDtypeStruct((SHARDS, 2, LANES), F32),
        in_specs=[VMEM],
        out_specs=VMEM,
        scratch_shapes=[pltpu.VMEM((TASKS * TASKS, LANES), F32)],
        compiler_params=pltpu.CompilerParams(vmem_limit_bytes=48 * 1024 * 1024),
    )(owned)
    gram = lax.all_to_all(gram, "shard", 0, 0)
    gram = call(sum_kernel, gram_blocks)(in_specs=[VMEM])(gram)
    gram = lax.all_to_all(gram, "task", 0, 0)
    out = jax.ShapeDtypeStruct((1, RANK, LOCAL), F32)
    return pl.pallas_call(
        combine_kernel,
        out_shape=(out, out),
        in_specs=[VMEM] * 4,
        out_specs=(VMEM, VMEM),
        scratch_shapes=[pltpu.VMEM((TASKS, TASKS, LANES), F32), pltpu.VMEM((TASKS, LANES), F32)],
        compiler_params=pltpu.CompilerParams(vmem_limit_bytes=48 * 1024 * 1024),
    )(gram, owned, orders, active)


def solution(mesh):
    placed = (
        P("shard", None),
        P("task", "shard", None),
        P("task", None),
        P("shard", None),
        P("shard", None),
        P(),
        P(),
    )
    return jax.shard_map(
        per_device,
        mesh=mesh,
        in_specs=placed,
        out_specs=(P("task", None, "shard"), P("task", None, "shard")),
        check_vma=False,
    )
```

```python
import functools

import jax
import jax.numpy as jnp
from jax import lax
from jax.experimental import pallas as pl
from jax.experimental.pallas import tpu as pltpu
from jax.sharding import PartitionSpec as P

EXPERTS = 16
RANK = 32
TOKENS = 512
TASKS = 16
SHARDS = 32
LOCAL = 144
LANES = 128
TAIL = LOCAL - LANES
TILES = 2 * RANK // 8 + 1
VMEM = pl.BlockSpec(memory_space=pltpu.VMEM)
HBM = pl.BlockSpec(memory_space=pltpu.HBM)
F32 = jnp.float32
BF16 = jnp.bfloat16


def call(kernel, out_shapes):
    return functools.partial(
        pl.pallas_call,
        kernel,
        out_shape=out_shapes,
        out_specs=jax.tree.map(lambda _: VMEM, out_shapes),
        compiler_params=pltpu.CompilerParams(vmem_limit_bytes=48 * 1024 * 1024),
    )


def over_features(factor, tokens):
    return lax.dot_general(
        factor, tokens, (((0,), (0,)), ((), ())), preferred_element_type=F32
    )


def lane_columns(square):
    row = lax.broadcasted_iota(jnp.int32, (TASKS, LANES), 0)
    lane = lax.broadcasted_iota(jnp.int32, (TASKS, LANES), 1)
    out = jnp.zeros((TASKS, LANES), square.dtype)
    for s in range(TASKS):
        column = jnp.broadcast_to(square[:, s : s + 1], out.shape)
        line = jnp.sum(jnp.where(row == lane, column, 0), axis=0, keepdims=True)
        out = jnp.where(row == s, line, out)
    return out


def encode_kernel(
    x_hbm,
    c_hbm,
    routes_hbm,
    down_hbm,
    up_hbm,
    order_hbm,
    conflict_hbm,
    out_ref,
    order_out,
    active_out,
    x_ref,
    c_ref,
    routes_ref,
    down_ref,
    up_ref,
    order_ref,
    conflict_ref,
    sems,
):
    pairs = (
        (routes_hbm, routes_ref),
        (x_hbm, x_ref),
        (down_hbm, down_ref),
        (c_hbm, c_ref),
        (up_hbm, up_ref),
        (order_hbm, order_ref),
        (conflict_hbm, conflict_ref),
    )
    copies = [pltpu.make_async_copy(src, dst, sems.at[i]) for i, (src, dst) in enumerate(pairs)]
    for copy in copies:
        copy.start()
    copies[5].wait()
    copies[6].wait()
    row = lax.broadcasted_iota(jnp.int32, (TASKS, LANES), 0)
    lane = lax.broadcasted_iota(jnp.int32, (TASKS, LANES), 1)
    orders = lane_columns(order_ref[...])
    conflicts = jnp.where(row == lane, 0, lane_columns(conflict_ref[...]))
    active = jnp.zeros((TASKS, LANES), jnp.int32)
    for j in range(TASKS):
        active = jnp.where(orders == j, conflicts[j : j + 1, :], active)
    order_out[...] = orders
    active_out[...] = jnp.where(lane < TASKS, active, 0).astype(F32)
    copies[0].wait()
    route = routes_ref[...]
    for part, (tokens, factor) in enumerate(((x_ref, down_ref), (c_ref, up_ref))):
        copies[1 + 2 * part].wait()
        copies[2 + 2 * part].wait()
        full = over_features(factor[...], tokens[...])
        picked = jnp.zeros((RANK, TOKENS), F32)
        for e in range(EXPERTS):
            picked = picked + jnp.where(route == e, full[e * RANK : (e + 1) * RANK, :], 0.0)
        for i in range(4):
            for q in range(4):
                out_ref[part * 16 + i * 4 + q] = picked[8 * i : 8 * i + 8, q * LANES : (q + 1) * LANES]


def sum_kernel(y_ref, out_ref):
    total = y_ref[0]
    for s in range(1, y_ref.shape[0]):
        total = total + y_ref[s]
    out_ref[...] = jnp.broadcast_to(total[None], out_ref.shape)


def grad_kernel(y_ref, x_ref, c_ref, routes_ref, out_ref):
    route = jnp.broadcast_to(routes_ref[...], (RANK, TOKENS))
    onehot = [jnp.where(route == e, 1.0, 0.0).astype(BF16) for e in range(EXPERTS)]
    pad = jnp.zeros((2 * LANES - LOCAL, TOKENS), BF16)
    for part, tokens in enumerate((c_ref, x_ref)):
        values = 2.0 * jnp.concatenate(
            [
                jnp.concatenate([y_ref[part * 16 + i * 4 + q] for q in range(4)], axis=1)
                for i in range(4)
            ],
            axis=0,
        )
        feats = jnp.concatenate([tokens[...], pad], axis=0)
        high = values.astype(BF16)
        low = (values - high.astype(F32)).astype(BF16)
        high = jnp.concatenate([high * hot for hot in onehot], axis=0)
        low = jnp.concatenate([low * hot for hot in onehot], axis=0)
        dims = (((1,), (1,)), ((), ()))
        grad = lax.dot_general(high, feats, dims, preferred_element_type=F32) + lax.dot_general(
            low, feats, dims, preferred_element_type=F32
        )
        first = RANK * (1 - part)
        for e in range(EXPERTS):
            tail = jnp.zeros((8, LANES), F32)
            for i in range(4):
                slot = first // 8 + i
                rows = slice(e * RANK + 8 * i, e * RANK + 8 * i + 8)
                out_ref[e, :, slot * LANES : (slot + 1) * LANES] = grad[rows, :LANES]
                piece = grad[rows, LANES:]
                tail = tail + (pltpu.roll(piece, slot * TAIL, 1) if slot else piece)
            if part == 0:
                out_ref[e, :, (TILES - 1) * LANES :] = tail
            else:
                out_ref[e, :, (TILES - 1) * LANES :] += tail


def gram_row(t, u):
    at = t // 8 * LANES + (7 - t % 8) * TASKS + u
    return slice(at, at + 1)


def gram_kernel(r_ref, out_ref, rows_ref):
    for t in range(TASKS):
        mine = [r_ref[t, :, k * LANES : (k + 1) * LANES] for k in range(TILES)]
        for u in range(t, TASKS):
            dot = mine[0] * r_ref[u, :, :LANES]
            for k in range(1, TILES):
                dot = dot + mine[k] * r_ref[u, :, k * LANES : (k + 1) * LANES]
            dot = jnp.sum(dot, axis=0, keepdims=True)
            rows_ref[gram_row(t, u)] = dot
            if u > t:
                rows_ref[gram_row(u, t)] = dot
    rest = rows_ref[...]
    lines = jnp.zeros((8, 2 * LANES), F32)
    for _ in range(3):
        piece = rest.astype(BF16)
        rest = rest - piece.astype(F32)
        lines = lines + lax.dot_general(
            jnp.ones((8, LANES), BF16), piece, (((1,), (1,)), ((), ())), preferred_element_type=F32
        )
    for half in range(2):
        line = lines[:1, half * LANES : (half + 1) * LANES]
        out_ref[:, half : half + 1, :] = jnp.broadcast_to(line[None], (TASKS, 1, LANES))


def combine_kernel(g_ref, r_ref, order_ref, active_ref, down_ref, up_ref, partner_ref, scale_ref):
    row = lax.broadcasted_iota(jnp.int32, (TASKS, LANES), 0)
    lane = lax.broadcasted_iota(jnp.int32, (TASKS, LANES), 1)
    lines = g_ref[0]
    for s in range(1, SHARDS):
        lines = lines + g_ref[s]
    gram = jnp.concatenate(
        [
            pltpu.roll(
                jnp.broadcast_to(lines[i : i + 1, :], (8, LANES)), TASKS, 1, stride=TASKS, stride_axis=0
            )
            for i in range(2)
        ],
        axis=0,
    )
    orders = order_ref[...]
    norm = jnp.sum(jnp.where(row == lane, gram, 0.0), axis=0, keepdims=True)
    norm = jnp.take_along_axis(jnp.broadcast_to(norm, gram.shape), orders, axis=1)
    scale_ref[...] = active_ref[...] / (norm + 1e-06)
    for k in range(TASKS):
        line = jnp.broadcast_to(gram[k : k + 1, :], gram.shape)
        partner_ref[k] = jnp.take_along_axis(line, orders, axis=1)
    full = (8, LANES)
    coef = [jnp.where(lane[:8] == k, 1.0, 0.0) for k in range(TASKS)]
    for s in range(TASKS):
        terms = [coef[k] * jnp.broadcast_to(partner_ref[k, s : s + 1, :], full) for k in range(TASKS)]
        while len(terms) > 1:
            terms = [a + b for a, b in zip(terms[::2], terms[1::2])]
        factor = jnp.broadcast_to(scale_ref[s : s + 1, :], full) * terms[0]
        pick = jnp.broadcast_to(order_ref[s : s + 1, :], full)
        coef = [coef[k] - jnp.where(pick == k, factor, 0.0) for k in range(TASKS)]
    total = None
    for t in range(TASKS):
        weight = jnp.sum(coef[t], axis=1, keepdims=True)[:1]
        term = weight * r_ref[t]
        total = term if total is None else total + term
    tail = total[:, (TILES - 1) * LANES :]
    for part, out in enumerate((down_ref, up_ref)):
        for i in range(4):
            slot = part * 4 + i
            out[0, 8 * i : 8 * i + 8, :LANES] = total[:, slot * LANES : (slot + 1) * LANES]
            piece = pltpu.roll(tail, LANES - slot * TAIL, 1) if slot else tail
            out[0, 8 * i : 8 * i + 8, LANES:] = piece[:, :TAIL]


def per_device(inputs, cotangent, routes, down_factor, up_factor, order, conflict):
    cot = cotangent[0]
    blocks = jax.ShapeDtypeStruct((SHARDS, 8, LANES), F32)
    gram_blocks = jax.ShapeDtypeStruct((SHARDS, 2, LANES), F32)
    plan = (
        jax.ShapeDtypeStruct((TASKS, LANES), jnp.int32),
        jax.ShapeDtypeStruct((TASKS, LANES), F32),
    )
    partial, orders, active = pl.pallas_call(
        encode_kernel,
        out_shape=(blocks, *plan),
        in_specs=[HBM] * 7,
        out_specs=(VMEM,) * 3,
        scratch_shapes=[
            pltpu.VMEM((LOCAL, TOKENS), BF16),
            pltpu.VMEM((LOCAL, TOKENS), BF16),
            pltpu.VMEM((1, TOKENS), jnp.int32),
            pltpu.VMEM((LOCAL, TOKENS), BF16),
            pltpu.VMEM((LOCAL, TOKENS), BF16),
            pltpu.VMEM((TASKS, TASKS), jnp.int32),
            pltpu.VMEM((TASKS, TASKS), jnp.int32),
            pltpu.SemaphoreType.DMA((7,)),
        ],
        compiler_params=pltpu.CompilerParams(vmem_limit_bytes=48 * 1024 * 1024),
    )(*(pltpu.with_memory_space_constraint(a, pltpu.HBM) for a in (inputs, cot, routes, down_factor, up_factor, order, conflict)))
    pieces = lax.all_to_all(partial, "shard", 0, 0)
    mine = call(sum_kernel, blocks)(in_specs=[VMEM])(pieces)
    codes = lax.all_to_all(mine, "shard", 0, 0)
    grads = call(grad_kernel, jax.ShapeDtypeStruct((EXPERTS, 8, TILES * LANES), F32))(in_specs=[VMEM] * 4)(
        codes, inputs, cot, routes
    )
    owned = lax.all_to_all(grads, "task", 0, 0)
    gram = pl.pallas_call(
        gram_kernel,
        out_shape=jax.ShapeDtypeStruct((TASKS, 2, LANES), F32),
        in_specs=[VMEM],
        out_specs=VMEM,
        scratch_shapes=[pltpu.VMEM((TASKS * TASKS, LANES), F32)],
        compiler_params=pltpu.CompilerParams(vmem_limit_bytes=48 * 1024 * 1024),
    )(owned)
    gram = lax.all_to_all(gram, "task", 0, 0)
    gram = call(sum_kernel, gram_blocks)(in_specs=[VMEM])(gram)
    gram = lax.all_to_all(gram, "shard", 0, 0)
    out = jax.ShapeDtypeStruct((1, RANK, LOCAL), F32)
    return pl.pallas_call(
        combine_kernel,
        out_shape=(out, out),
        in_specs=[VMEM] * 4,
        out_specs=(VMEM, VMEM),
        scratch_shapes=[pltpu.VMEM((TASKS, TASKS, LANES), F32), pltpu.VMEM((TASKS, LANES), F32)],
        compiler_params=pltpu.CompilerParams(vmem_limit_bytes=48 * 1024 * 1024),
    )(gram, owned, orders, active)


def solution(mesh):
    placed = (
        P("shard", None),
        P("task", "shard", None),
        P("task", None),
        P("shard", None),
        P("shard", None),
        P(),
        P(),
    )
    return jax.shard_map(
        per_device,
        mesh=mesh,
        in_specs=placed,
        out_specs=(P("task", None, "shard"), P("task", None, "shard")),
        check_vma=False,
    )
```

```python
import functools

import jax
import jax.numpy as jnp
from jax import lax
from jax.experimental import pallas as pl
from jax.experimental.pallas import tpu as pltpu
from jax.sharding import PartitionSpec as P

EXPERTS = 16
RANK = 32
TOKENS = 512
TASKS = 16
SHARDS = 32
LOCAL = 144
LANES = 128
TAIL = LOCAL - LANES
TILES = 2 * RANK // 8 + 1
VMEM = pl.BlockSpec(memory_space=pltpu.VMEM)
HBM = pl.BlockSpec(memory_space=pltpu.HBM)
F32 = jnp.float32
BF16 = jnp.bfloat16


def call(kernel, out_shapes):
    return functools.partial(
        pl.pallas_call,
        kernel,
        out_shape=out_shapes,
        out_specs=jax.tree.map(lambda _: VMEM, out_shapes),
        compiler_params=pltpu.CompilerParams(vmem_limit_bytes=48 * 1024 * 1024),
    )


def over_features(factor, tokens):
    return lax.dot_general(
        factor, tokens, (((0,), (0,)), ((), ())), preferred_element_type=F32
    )


def lane_columns(square):
    row = lax.broadcasted_iota(jnp.int32, (TASKS, LANES), 0)
    lane = lax.broadcasted_iota(jnp.int32, (TASKS, LANES), 1)
    out = jnp.zeros((TASKS, LANES), square.dtype)
    for s in range(TASKS):
        column = jnp.broadcast_to(square[:, s : s + 1], out.shape)
        line = jnp.sum(jnp.where(row == lane, column, 0), axis=0, keepdims=True)
        out = jnp.where(row == s, line, out)
    return out


def encode_kernel(
    x_hbm,
    c_hbm,
    routes_hbm,
    down_hbm,
    up_hbm,
    order_hbm,
    conflict_hbm,
    out_ref,
    order_out,
    active_out,
    x_ref,
    c_ref,
    routes_ref,
    down_ref,
    up_ref,
    order_ref,
    conflict_ref,
    sems,
):
    pairs = (
        (routes_hbm, routes_ref),
        (x_hbm, x_ref),
        (down_hbm, down_ref),
        (c_hbm, c_ref),
        (up_hbm, up_ref),
        (order_hbm, order_ref),
        (conflict_hbm, conflict_ref),
    )
    copies = [pltpu.make_async_copy(src, dst, sems.at[i]) for i, (src, dst) in enumerate(pairs)]
    for copy in copies:
        copy.start()
    copies[5].wait()
    copies[6].wait()
    row = lax.broadcasted_iota(jnp.int32, (TASKS, LANES), 0)
    lane = lax.broadcasted_iota(jnp.int32, (TASKS, LANES), 1)
    orders = lane_columns(order_ref[...])
    conflicts = jnp.where(row == lane, 0, lane_columns(conflict_ref[...]))
    active = jnp.zeros((TASKS, LANES), jnp.int32)
    for j in range(TASKS):
        active = jnp.where(orders == j, conflicts[j : j + 1, :], active)
    order_out[...] = orders
    active_out[...] = jnp.where(lane < TASKS, active, 0).astype(F32)
    copies[0].wait()
    route = routes_ref[...]
    for part, (tokens, factor) in enumerate(((x_ref, down_ref), (c_ref, up_ref))):
        copies[1 + 2 * part].wait()
        copies[2 + 2 * part].wait()
        full = over_features(factor[...], tokens[...])
        picked = jnp.zeros((RANK, TOKENS), F32)
        for e in range(EXPERTS):
            picked = picked + jnp.where(route == e, full[e * RANK : (e + 1) * RANK, :], 0.0)
        for i in range(4):
            for q in range(4):
                out_ref[part * 16 + i * 4 + q] = picked[8 * i : 8 * i + 8, q * LANES : (q + 1) * LANES]


def half_kernel(y_ref, out_ref):
    half = SHARDS // 2
    first = lax.rem(lax.axis_index("shard"), 2) * half
    total = y_ref[0, pl.ds(first, half)] + y_ref[1, pl.ds(first, half)]
    out_ref[...] = jnp.broadcast_to(total[None], out_ref.shape)


def total_kernel(y_ref, out_ref):
    total = y_ref[0]
    for s in range(1, y_ref.shape[0]):
        total = total + y_ref[s]
    out_ref[...] = total


def sum_kernel(y_ref, out_ref):
    total = y_ref[0]
    for s in range(1, y_ref.shape[0]):
        total = total + y_ref[s]
    out_ref[...] = jnp.broadcast_to(total[None], out_ref.shape)


def grad_kernel(y_ref, x_ref, c_ref, routes_ref, out_ref):
    route = jnp.broadcast_to(routes_ref[...], (RANK, TOKENS))
    onehot = [jnp.where(route == e, 1.0, 0.0).astype(BF16) for e in range(EXPERTS)]
    pad = jnp.zeros((2 * LANES - LOCAL, TOKENS), BF16)
    for part, tokens in enumerate((c_ref, x_ref)):
        values = 2.0 * jnp.concatenate(
            [
                jnp.concatenate([y_ref[part * 16 + i * 4 + q] for q in range(4)], axis=1)
                for i in range(4)
            ],
            axis=0,
        )
        feats = jnp.concatenate([tokens[...], pad], axis=0)
        high = values.astype(BF16)
        low = (values - high.astype(F32)).astype(BF16)
        high = jnp.concatenate([high * hot for hot in onehot], axis=0)
        low = jnp.concatenate([low * hot for hot in onehot], axis=0)
        dims = (((1,), (1,)), ((), ()))
        grad = lax.dot_general(high, feats, dims, preferred_element_type=F32) + lax.dot_general(
            low, feats, dims, preferred_element_type=F32
        )
        first = RANK * (1 - part)
        for e in range(EXPERTS):
            tail = jnp.zeros((8, LANES), F32)
            for i in range(4):
                slot = first // 8 + i
                rows = slice(e * RANK + 8 * i, e * RANK + 8 * i + 8)
                out_ref[e, :, slot * LANES : (slot + 1) * LANES] = grad[rows, :LANES]
                piece = grad[rows, LANES:]
                tail = tail + (pltpu.roll(piece, slot * TAIL, 1) if slot else piece)
            if part == 0:
                out_ref[e, :, (TILES - 1) * LANES :] = tail
            else:
                out_ref[e, :, (TILES - 1) * LANES :] += tail


def gram_row(t, u):
    at = t // 8 * LANES + (7 - t % 8) * TASKS + u
    return slice(at, at + 1)


def gram_kernel(r_ref, out_ref, rows_ref):
    for t in range(TASKS):
        mine = [r_ref[t, :, k * LANES : (k + 1) * LANES] for k in range(TILES)]
        for u in range(t, TASKS):
            dot = mine[0] * r_ref[u, :, :LANES]
            for k in range(1, TILES):
                dot = dot + mine[k] * r_ref[u, :, k * LANES : (k + 1) * LANES]
            dot = jnp.sum(dot, axis=0, keepdims=True)
            rows_ref[gram_row(t, u)] = dot
            if u > t:
                rows_ref[gram_row(u, t)] = dot
    rest = rows_ref[...]
    lines = jnp.zeros((8, 2 * LANES), F32)
    for _ in range(3):
        piece = rest.astype(BF16)
        rest = rest - piece.astype(F32)
        lines = lines + lax.dot_general(
            jnp.ones((8, LANES), BF16), piece, (((1,), (1,)), ((), ())), preferred_element_type=F32
        )
    for half in range(2):
        line = lines[:1, half * LANES : (half + 1) * LANES]
        out_ref[:, half : half + 1, :] = jnp.broadcast_to(line[None], (SHARDS, 1, LANES))


def combine_kernel(g_ref, r_ref, order_ref, active_ref, down_ref, up_ref, partner_ref, scale_ref):
    row = lax.broadcasted_iota(jnp.int32, (TASKS, LANES), 0)
    lane = lax.broadcasted_iota(jnp.int32, (TASKS, LANES), 1)
    lines = g_ref[0]
    for t in range(1, TASKS):
        lines = lines + g_ref[t]
    gram = jnp.concatenate(
        [
            pltpu.roll(
                jnp.broadcast_to(lines[i : i + 1, :], (8, LANES)), TASKS, 1, stride=TASKS, stride_axis=0
            )
            for i in range(2)
        ],
        axis=0,
    )
    orders = order_ref[...]
    norm = jnp.sum(jnp.where(row == lane, gram, 0.0), axis=0, keepdims=True)
    norm = jnp.take_along_axis(jnp.broadcast_to(norm, gram.shape), orders, axis=1)
    scale_ref[...] = active_ref[...] / (norm + 1e-06)
    for k in range(TASKS):
        line = jnp.broadcast_to(gram[k : k + 1, :], gram.shape)
        partner_ref[k] = jnp.take_along_axis(line, orders, axis=1)
    full = (8, LANES)
    coef = [jnp.where(lane[:8] == k, 1.0, 0.0) for k in range(TASKS)]
    for s in range(TASKS):
        terms = [coef[k] * jnp.broadcast_to(partner_ref[k, s : s + 1, :], full) for k in range(TASKS)]
        while len(terms) > 1:
            terms = [a + b for a, b in zip(terms[::2], terms[1::2])]
        factor = jnp.broadcast_to(scale_ref[s : s + 1, :], full) * terms[0]
        pick = jnp.broadcast_to(order_ref[s : s + 1, :], full)
        coef = [coef[k] - jnp.where(pick == k, factor, 0.0) for k in range(TASKS)]
    total = None
    for t in range(TASKS):
        weight = jnp.sum(coef[t], axis=1, keepdims=True)[:1]
        term = weight * r_ref[t]
        total = term if total is None else total + term
    tail = total[:, (TILES - 1) * LANES :]
    for part, out in enumerate((down_ref, up_ref)):
        for i in range(4):
            slot = part * 4 + i
            out[0, 8 * i : 8 * i + 8, :LANES] = total[:, slot * LANES : (slot + 1) * LANES]
            piece = pltpu.roll(tail, LANES - slot * TAIL, 1) if slot else tail
            out[0, 8 * i : 8 * i + 8, LANES:] = piece[:, :TAIL]


def per_device(inputs, cotangent, routes, down_factor, up_factor, order, conflict):
    cot = cotangent[0]
    blocks = jax.ShapeDtypeStruct((SHARDS, 8, LANES), F32)
    gram_blocks = jax.ShapeDtypeStruct((TASKS, 2, LANES), F32)
    plan = (
        jax.ShapeDtypeStruct((TASKS, LANES), jnp.int32),
        jax.ShapeDtypeStruct((TASKS, LANES), F32),
    )
    partial, orders, active = pl.pallas_call(
        encode_kernel,
        out_shape=(blocks, *plan),
        in_specs=[HBM] * 7,
        out_specs=(VMEM,) * 3,
        scratch_shapes=[
            pltpu.VMEM((LOCAL, TOKENS), BF16),
            pltpu.VMEM((LOCAL, TOKENS), BF16),
            pltpu.VMEM((1, TOKENS), jnp.int32),
            pltpu.VMEM((LOCAL, TOKENS), BF16),
            pltpu.VMEM((LOCAL, TOKENS), BF16),
            pltpu.VMEM((TASKS, TASKS), jnp.int32),
            pltpu.VMEM((TASKS, TASKS), jnp.int32),
            pltpu.SemaphoreType.DMA((7,)),
        ],
        compiler_params=pltpu.CompilerParams(vmem_limit_bytes=48 * 1024 * 1024),
    )(*(pltpu.with_memory_space_constraint(a, pltpu.HBM) for a in (inputs, cot, routes, down_factor, up_factor, order, conflict)))
    half = SHARDS // 2
    chips = [[2 * i, 2 * i + 1] for i in range(half)]
    cores = [[2 * i + c for i in range(half)] for c in range(2)]
    pair = lax.all_gather(partial, "shard", axis_index_groups=chips)
    mine = call(half_kernel, jax.ShapeDtypeStruct((half, half, 8, LANES), F32))(in_specs=[VMEM])(pair)
    pieces = lax.all_to_all(mine, "shard", 0, 0, axis_index_groups=cores)
    mine = call(total_kernel, jax.ShapeDtypeStruct((half, 8, LANES), F32))(in_specs=[VMEM])(pieces)
    codes = lax.all_gather(mine, "shard", axis_index_groups=chips).reshape(SHARDS, 8, LANES)
    grads = call(grad_kernel, jax.ShapeDtypeStruct((EXPERTS, 8, TILES * LANES), F32))(in_specs=[VMEM] * 4)(
        codes, inputs, cot, routes
    )
    owned = lax.all_to_all(grads, "task", 0, 0)
    gram = pl.pallas_call(
        gram_kernel,
        out_shape=jax.ShapeDtypeStruct((SHARDS, 2, LANES), F32),
        in_specs=[VMEM],
        out_specs=VMEM,
        scratch_shapes=[pltpu.VMEM((TASKS * TASKS, LANES), F32)],
        compiler_params=pltpu.CompilerParams(vmem_limit_bytes=48 * 1024 * 1024),
    )(owned)
    gram = lax.all_to_all(gram, "shard", 0, 0)
    gram = call(sum_kernel, gram_blocks)(in_specs=[VMEM])(gram)
    gram = lax.all_to_all(gram, "task", 0, 0)
    out = jax.ShapeDtypeStruct((1, RANK, LOCAL), F32)
    return pl.pallas_call(
        combine_kernel,
        out_shape=(out, out),
        in_specs=[VMEM] * 4,
        out_specs=(VMEM, VMEM),
        scratch_shapes=[pltpu.VMEM((TASKS, TASKS, LANES), F32), pltpu.VMEM((TASKS, LANES), F32)],
        compiler_params=pltpu.CompilerParams(vmem_limit_bytes=48 * 1024 * 1024),
    )(gram, owned, orders, active)


def solution(mesh):
    placed = (
        P("shard", None),
        P("task", "shard", None),
        P("task", None),
        P("shard", None),
        P("shard", None),
        P(),
        P(),
    )
    return jax.shard_map(
        per_device,
        mesh=mesh,
        in_specs=placed,
        out_specs=(P("task", None, "shard"), P("task", None, "shard")),
        check_vma=False,
    )
```

```python
import functools

import jax
import jax.numpy as jnp
from jax import lax
from jax.experimental import pallas as pl
from jax.experimental.pallas import tpu as pltpu
from jax.sharding import Mesh
from jax.sharding import PartitionSpec as P

EXPERTS = 16
RANK = 32
TOKENS = 512
TASKS = 16
SHARDS = 32
LOCAL = 144
LANES = 128
TAIL = LOCAL - LANES
TILES = 2 * RANK // 8 + 1
VMEM = pl.BlockSpec(memory_space=pltpu.VMEM)
HBM = pl.BlockSpec(memory_space=pltpu.HBM)
F32 = jnp.float32
BF16 = jnp.bfloat16


def call(kernel, out_shapes):
    return functools.partial(
        pl.pallas_call,
        kernel,
        out_shape=out_shapes,
        out_specs=jax.tree.map(lambda _: VMEM, out_shapes),
        compiler_params=pltpu.CompilerParams(vmem_limit_bytes=48 * 1024 * 1024),
    )


def over_features(factor, tokens):
    return lax.dot_general(
        factor, tokens, (((0,), (0,)), ((), ())), preferred_element_type=F32
    )


def lane_columns(square):
    row = lax.broadcasted_iota(jnp.int32, (TASKS, LANES), 0)
    lane = lax.broadcasted_iota(jnp.int32, (TASKS, LANES), 1)
    out = jnp.zeros((TASKS, LANES), square.dtype)
    for s in range(TASKS):
        column = jnp.broadcast_to(square[:, s : s + 1], out.shape)
        line = jnp.sum(jnp.where(row == lane, column, 0), axis=0, keepdims=True)
        out = jnp.where(row == s, line, out)
    return out


def encode_kernel(
    x_hbm,
    c_hbm,
    routes_hbm,
    down_hbm,
    up_hbm,
    order_hbm,
    conflict_hbm,
    out_ref,
    order_out,
    active_out,
    x_ref,
    c_ref,
    routes_ref,
    down_ref,
    up_ref,
    order_ref,
    conflict_ref,
    sems,
):
    pairs = (
        (routes_hbm, routes_ref),
        (x_hbm, x_ref),
        (down_hbm, down_ref),
        (c_hbm, c_ref),
        (up_hbm, up_ref),
        (order_hbm, order_ref),
        (conflict_hbm, conflict_ref),
    )
    copies = [pltpu.make_async_copy(src, dst, sems.at[i]) for i, (src, dst) in enumerate(pairs)]
    for copy in copies:
        copy.start()
    copies[5].wait()
    copies[6].wait()
    row = lax.broadcasted_iota(jnp.int32, (TASKS, LANES), 0)
    lane = lax.broadcasted_iota(jnp.int32, (TASKS, LANES), 1)
    orders = lane_columns(order_ref[...])
    conflicts = jnp.where(row == lane, 0, lane_columns(conflict_ref[...]))
    active = jnp.zeros((TASKS, LANES), jnp.int32)
    for j in range(TASKS):
        active = jnp.where(orders == j, conflicts[j : j + 1, :], active)
    order_out[...] = orders
    active_out[...] = jnp.where(lane < TASKS, active, 0).astype(F32)
    copies[0].wait()
    route = routes_ref[...]
    for part, (tokens, factor) in enumerate(((x_ref, down_ref), (c_ref, up_ref))):
        copies[1 + 2 * part].wait()
        copies[2 + 2 * part].wait()
        full = over_features(factor[...], tokens[...])
        picked = jnp.zeros((RANK, TOKENS), F32)
        for e in range(EXPERTS):
            picked = picked + jnp.where(route == e, full[e * RANK : (e + 1) * RANK, :], 0.0)
        for i in range(4):
            for q in range(4):
                out_ref[part * 16 + i * 4 + q] = picked[8 * i : 8 * i + 8, q * LANES : (q + 1) * LANES]


def half_kernel(y_ref, out_ref):
    half = SHARDS // 2
    first = lax.axis_index("core") * half
    total = y_ref[0, pl.ds(first, half)] + y_ref[1, pl.ds(first, half)]
    out_ref[...] = jnp.broadcast_to(total[None], out_ref.shape)


def total_kernel(y_ref, out_ref):
    total = y_ref[0]
    for s in range(1, y_ref.shape[0]):
        total = total + y_ref[s]
    out_ref[...] = total


def sum_kernel(y_ref, out_ref):
    total = y_ref[0]
    for s in range(1, y_ref.shape[0]):
        total = total + y_ref[s]
    out_ref[...] = jnp.broadcast_to(total[None], out_ref.shape)


def grad_kernel(y_ref, x_ref, c_ref, routes_ref, out_ref):
    route = jnp.broadcast_to(routes_ref[...], (RANK, TOKENS))
    onehot = [jnp.where(route == e, 1.0, 0.0).astype(BF16) for e in range(EXPERTS)]
    pad = jnp.zeros((2 * LANES - LOCAL, TOKENS), BF16)
    for part, tokens in enumerate((c_ref, x_ref)):
        values = 2.0 * jnp.concatenate(
            [
                jnp.concatenate([y_ref[part * 16 + i * 4 + q] for q in range(4)], axis=1)
                for i in range(4)
            ],
            axis=0,
        )
        feats = jnp.concatenate([tokens[...], pad], axis=0)
        high = values.astype(BF16)
        low = (values - high.astype(F32)).astype(BF16)
        high = jnp.concatenate([high * hot for hot in onehot], axis=0)
        low = jnp.concatenate([low * hot for hot in onehot], axis=0)
        dims = (((1,), (1,)), ((), ()))
        grad = lax.dot_general(high, feats, dims, preferred_element_type=F32) + lax.dot_general(
            low, feats, dims, preferred_element_type=F32
        )
        first = RANK * (1 - part)
        for e in range(EXPERTS):
            tail = jnp.zeros((8, LANES), F32)
            for i in range(4):
                slot = first // 8 + i
                rows = slice(e * RANK + 8 * i, e * RANK + 8 * i + 8)
                out_ref[e, :, slot * LANES : (slot + 1) * LANES] = grad[rows, :LANES]
                piece = grad[rows, LANES:]
                tail = tail + (pltpu.roll(piece, slot * TAIL, 1) if slot else piece)
            if part == 0:
                out_ref[e, :, (TILES - 1) * LANES :] = tail
            else:
                out_ref[e, :, (TILES - 1) * LANES :] += tail


def gram_row(t, u):
    at = t // 8 * LANES + (7 - t % 8) * TASKS + u
    return slice(at, at + 1)


def gram_kernel(r_ref, out_ref, rows_ref):
    for t in range(TASKS):
        mine = [r_ref[t, :, k * LANES : (k + 1) * LANES] for k in range(TILES)]
        for u in range(t, TASKS):
            dot = mine[0] * r_ref[u, :, :LANES]
            for k in range(1, TILES):
                dot = dot + mine[k] * r_ref[u, :, k * LANES : (k + 1) * LANES]
            dot = jnp.sum(dot, axis=0, keepdims=True)
            rows_ref[gram_row(t, u)] = dot
            if u > t:
                rows_ref[gram_row(u, t)] = dot
    rest = rows_ref[...]
    lines = jnp.zeros((8, 2 * LANES), F32)
    for _ in range(3):
        piece = rest.astype(BF16)
        rest = rest - piece.astype(F32)
        lines = lines + lax.dot_general(
            jnp.ones((8, LANES), BF16), piece, (((1,), (1,)), ((), ())), preferred_element_type=F32
        )
    for half in range(2):
        line = lines[:1, half * LANES : (half + 1) * LANES]
        out_ref[:, half : half + 1, :] = jnp.broadcast_to(line[None], (SHARDS, 1, LANES))


def combine_kernel(g_ref, r_ref, order_ref, active_ref, down_ref, up_ref, partner_ref, scale_ref):
    row = lax.broadcasted_iota(jnp.int32, (TASKS, LANES), 0)
    lane = lax.broadcasted_iota(jnp.int32, (TASKS, LANES), 1)
    lines = g_ref[0]
    for t in range(1, TASKS):
        lines = lines + g_ref[t]
    gram = jnp.concatenate(
        [
            pltpu.roll(
                jnp.broadcast_to(lines[i : i + 1, :], (8, LANES)), TASKS, 1, stride=TASKS, stride_axis=0
            )
            for i in range(2)
        ],
        axis=0,
    )
    orders = order_ref[...]
    norm = jnp.sum(jnp.where(row == lane, gram, 0.0), axis=0, keepdims=True)
    norm = jnp.take_along_axis(jnp.broadcast_to(norm, gram.shape), orders, axis=1)
    scale_ref[...] = active_ref[...] / (norm + 1e-06)
    for k in range(TASKS):
        line = jnp.broadcast_to(gram[k : k + 1, :], gram.shape)
        partner_ref[k] = jnp.take_along_axis(line, orders, axis=1)
    full = (8, LANES)
    coef = [jnp.where(lane[:8] == k, 1.0, 0.0) for k in range(TASKS)]
    for s in range(TASKS):
        terms = [coef[k] * jnp.broadcast_to(partner_ref[k, s : s + 1, :], full) for k in range(TASKS)]
        while len(terms) > 1:
            terms = [a + b for a, b in zip(terms[::2], terms[1::2])]
        factor = jnp.broadcast_to(scale_ref[s : s + 1, :], full) * terms[0]
        pick = jnp.broadcast_to(order_ref[s : s + 1, :], full)
        coef = [coef[k] - jnp.where(pick == k, factor, 0.0) for k in range(TASKS)]
    total = None
    for t in range(TASKS):
        weight = jnp.sum(coef[t], axis=1, keepdims=True)[:1]
        term = weight * r_ref[t]
        total = term if total is None else total + term
    tail = total[:, (TILES - 1) * LANES :]
    for part, out in enumerate((down_ref, up_ref)):
        for i in range(4):
            slot = part * 4 + i
            out[0, 8 * i : 8 * i + 8, :LANES] = total[:, slot * LANES : (slot + 1) * LANES]
            piece = pltpu.roll(tail, LANES - slot * TAIL, 1) if slot else tail
            out[0, 8 * i : 8 * i + 8, LANES:] = piece[:, :TAIL]


def per_device(inputs, cotangent, routes, down_factor, up_factor, order, conflict):
    cot = cotangent[0]
    blocks = jax.ShapeDtypeStruct((SHARDS, 8, LANES), F32)
    gram_blocks = jax.ShapeDtypeStruct((TASKS, 2, LANES), F32)
    plan = (
        jax.ShapeDtypeStruct((TASKS, LANES), jnp.int32),
        jax.ShapeDtypeStruct((TASKS, LANES), F32),
    )
    partial, orders, active = pl.pallas_call(
        encode_kernel,
        out_shape=(blocks, *plan),
        in_specs=[HBM] * 7,
        out_specs=(VMEM,) * 3,
        scratch_shapes=[
            pltpu.VMEM((LOCAL, TOKENS), BF16),
            pltpu.VMEM((LOCAL, TOKENS), BF16),
            pltpu.VMEM((1, TOKENS), jnp.int32),
            pltpu.VMEM((LOCAL, TOKENS), BF16),
            pltpu.VMEM((LOCAL, TOKENS), BF16),
            pltpu.VMEM((TASKS, TASKS), jnp.int32),
            pltpu.VMEM((TASKS, TASKS), jnp.int32),
            pltpu.SemaphoreType.DMA((7,)),
        ],
        compiler_params=pltpu.CompilerParams(vmem_limit_bytes=48 * 1024 * 1024),
    )(*(pltpu.with_memory_space_constraint(a, pltpu.HBM) for a in (inputs, cot, routes, down_factor, up_factor, order, conflict)))
    half = SHARDS // 2
    pair = lax.all_gather(partial, "core")
    mine = call(half_kernel, jax.ShapeDtypeStruct((half, half, 8, LANES), F32))(in_specs=[VMEM])(pair)
    pieces = lax.all_to_all(mine, "chip", 0, 0)
    mine = call(total_kernel, jax.ShapeDtypeStruct((half, 8, LANES), F32))(in_specs=[VMEM])(pieces)
    codes = lax.all_gather(mine, "core").reshape(SHARDS, 8, LANES)
    grads = call(grad_kernel, jax.ShapeDtypeStruct((EXPERTS, 8, TILES * LANES), F32))(in_specs=[VMEM] * 4)(
        codes, inputs, cot, routes
    )
    owned = lax.all_to_all(grads, "task", 0, 0)
    gram = pl.pallas_call(
        gram_kernel,
        out_shape=jax.ShapeDtypeStruct((SHARDS, 2, LANES), F32),
        in_specs=[VMEM],
        out_specs=VMEM,
        scratch_shapes=[pltpu.VMEM((TASKS * TASKS, LANES), F32)],
        compiler_params=pltpu.CompilerParams(vmem_limit_bytes=48 * 1024 * 1024),
    )(owned)
    gram = lax.all_to_all(gram, ("chip", "core"), 0, 0)
    gram = call(sum_kernel, gram_blocks)(in_specs=[VMEM])(gram)
    gram = lax.all_to_all(gram, "task", 0, 0)
    out = jax.ShapeDtypeStruct((1, RANK, LOCAL), F32)
    return pl.pallas_call(
        combine_kernel,
        out_shape=(out, out),
        in_specs=[VMEM] * 4,
        out_specs=(VMEM, VMEM),
        scratch_shapes=[pltpu.VMEM((TASKS, TASKS, LANES), F32), pltpu.VMEM((TASKS, LANES), F32)],
        compiler_params=pltpu.CompilerParams(vmem_limit_bytes=48 * 1024 * 1024),
    )(gram, owned, orders, active)


def solution(mesh):
    tasks, shards = mesh.devices.shape
    mesh = Mesh(mesh.devices.reshape(tasks, shards // 2, 2), ("task", "chip", "core"))
    shard = ("chip", "core")
    placed = (
        P(shard, None),
        P("task", shard, None),
        P("task", None),
        P(shard, None),
        P(shard, None),
        P(),
        P(),
    )
    return jax.shard_map(
        per_device,
        mesh=mesh,
        in_specs=placed,
        out_specs=(P("task", None, shard), P("task", None, shard)),
        check_vma=False,
    )
```

```python
import functools

import jax
import jax.numpy as jnp
from jax import lax
from jax.experimental import pallas as pl
from jax.experimental.pallas import tpu as pltpu
from jax.sharding import PartitionSpec as P

EXPERTS = 16
RANK = 32
TOKENS = 512
TASKS = 16
SHARDS = 32
LOCAL = 144
LANES = 128
TAIL = LOCAL - LANES
TILES = 2 * RANK // 8 + 1
VMEM = pl.BlockSpec(memory_space=pltpu.VMEM)
HBM = pl.BlockSpec(memory_space=pltpu.HBM)
F32 = jnp.float32
BF16 = jnp.bfloat16


def call(kernel, out_shapes):
    return functools.partial(
        pl.pallas_call,
        kernel,
        out_shape=out_shapes,
        out_specs=jax.tree.map(lambda _: VMEM, out_shapes),
        compiler_params=pltpu.CompilerParams(vmem_limit_bytes=48 * 1024 * 1024),
    )


def over_features(factor, tokens):
    return lax.dot_general(
        factor, tokens, (((0,), (0,)), ((), ())), preferred_element_type=F32
    )


def lane_columns(square):
    row = lax.broadcasted_iota(jnp.int32, (TASKS, LANES), 0)
    lane = lax.broadcasted_iota(jnp.int32, (TASKS, LANES), 1)
    out = jnp.zeros((TASKS, LANES), square.dtype)
    for s in range(TASKS):
        column = jnp.broadcast_to(square[:, s : s + 1], out.shape)
        line = jnp.sum(jnp.where(row == lane, column, 0), axis=0, keepdims=True)
        out = jnp.where(row == s, line, out)
    return out


def plan_kernel(order_ref, conflict_ref, after_ref, order_out, active_out):
    del after_ref
    row = lax.broadcasted_iota(jnp.int32, (TASKS, LANES), 0)
    lane = lax.broadcasted_iota(jnp.int32, (TASKS, LANES), 1)
    orders = lane_columns(order_ref[...])
    conflicts = jnp.where(row == lane, 0, lane_columns(conflict_ref[...]))
    active = jnp.zeros((TASKS, LANES), jnp.int32)
    for j in range(TASKS):
        active = jnp.where(orders == j, conflicts[j : j + 1, :], active)
    order_out[...] = orders
    active_out[...] = jnp.where(lane < TASKS, active, 0).astype(F32)


def encode_kernel(
    x_hbm,
    c_hbm,
    routes_hbm,
    down_hbm,
    up_hbm,
    out_ref,
    x_ref,
    c_ref,
    routes_ref,
    down_ref,
    up_ref,
    sems,
):
    pairs = (
        (routes_hbm, routes_ref),
        (x_hbm, x_ref),
        (down_hbm, down_ref),
        (c_hbm, c_ref),
        (up_hbm, up_ref),
    )
    copies = [pltpu.make_async_copy(src, dst, sems.at[i]) for i, (src, dst) in enumerate(pairs)]
    for copy in copies:
        copy.start()
    copies[0].wait()
    route = routes_ref[...]
    for part, (tokens, factor) in enumerate(((x_ref, down_ref), (c_ref, up_ref))):
        copies[1 + 2 * part].wait()
        copies[2 + 2 * part].wait()
        full = over_features(factor[...], tokens[...])
        picked = jnp.zeros((RANK, TOKENS), F32)
        for e in range(EXPERTS):
            picked = picked + jnp.where(route == e, full[e * RANK : (e + 1) * RANK, :], 0.0)
        for i in range(4):
            for q in range(4):
                out_ref[part * 16 + i * 4 + q] = picked[8 * i : 8 * i + 8, q * LANES : (q + 1) * LANES]


def sum_kernel(y_ref, out_ref):
    total = y_ref[0]
    for s in range(1, y_ref.shape[0]):
        total = total + y_ref[s]
    out_ref[...] = jnp.broadcast_to(total[None], out_ref.shape)


def grad_kernel(y_ref, x_ref, c_ref, routes_ref, out_ref, done_ref):
    done_ref[...] = jnp.zeros_like(done_ref)
    route = jnp.broadcast_to(routes_ref[...], (RANK, TOKENS))
    onehot = [jnp.where(route == e, 1.0, 0.0).astype(BF16) for e in range(EXPERTS)]
    pad = jnp.zeros((2 * LANES - LOCAL, TOKENS), BF16)
    for part, tokens in enumerate((c_ref, x_ref)):
        values = 2.0 * jnp.concatenate(
            [
                jnp.concatenate([y_ref[part * 16 + i * 4 + q] for q in range(4)], axis=1)
                for i in range(4)
            ],
            axis=0,
        )
        feats = jnp.concatenate([tokens[...], pad], axis=0)
        high = values.astype(BF16)
        low = (values - high.astype(F32)).astype(BF16)
        high = jnp.concatenate([high * hot for hot in onehot], axis=0)
        low = jnp.concatenate([low * hot for hot in onehot], axis=0)
        dims = (((1,), (1,)), ((), ()))
        grad = lax.dot_general(high, feats, dims, preferred_element_type=F32) + lax.dot_general(
            low, feats, dims, preferred_element_type=F32
        )
        first = RANK * (1 - part)
        for e in range(EXPERTS):
            tail = jnp.zeros((8, LANES), F32)
            for i in range(4):
                slot = first // 8 + i
                rows = slice(e * RANK + 8 * i, e * RANK + 8 * i + 8)
                out_ref[e, :, slot * LANES : (slot + 1) * LANES] = grad[rows, :LANES]
                piece = grad[rows, LANES:]
                tail = tail + (pltpu.roll(piece, slot * TAIL, 1) if slot else piece)
            if part == 0:
                out_ref[e, :, (TILES - 1) * LANES :] = tail
            else:
                out_ref[e, :, (TILES - 1) * LANES :] += tail


def gram_row(t, u):
    at = t // 8 * LANES + (7 - t % 8) * TASKS + u
    return slice(at, at + 1)


def gram_kernel(r_ref, out_ref, rows_ref):
    for t in range(TASKS):
        mine = [r_ref[t, :, k * LANES : (k + 1) * LANES] for k in range(TILES)]
        for u in range(t, TASKS):
            dot = mine[0] * r_ref[u, :, :LANES]
            for k in range(1, TILES):
                dot = dot + mine[k] * r_ref[u, :, k * LANES : (k + 1) * LANES]
            dot = jnp.sum(dot, axis=0, keepdims=True)
            rows_ref[gram_row(t, u)] = dot
            if u > t:
                rows_ref[gram_row(u, t)] = dot
    rest = rows_ref[...]
    lines = jnp.zeros((8, 2 * LANES), F32)
    for _ in range(3):
        piece = rest.astype(BF16)
        rest = rest - piece.astype(F32)
        lines = lines + lax.dot_general(
            jnp.ones((8, LANES), BF16), piece, (((1,), (1,)), ((), ())), preferred_element_type=F32
        )
    for half in range(2):
        line = lines[:1, half * LANES : (half + 1) * LANES]
        out_ref[:, half : half + 1, :] = jnp.broadcast_to(line[None], (SHARDS, 1, LANES))


def combine_kernel(g_ref, r_ref, order_ref, active_ref, down_ref, up_ref, partner_ref, scale_ref):
    row = lax.broadcasted_iota(jnp.int32, (TASKS, LANES), 0)
    lane = lax.broadcasted_iota(jnp.int32, (TASKS, LANES), 1)
    lines = g_ref[0]
    for t in range(1, TASKS):
        lines = lines + g_ref[t]
    gram = jnp.concatenate(
        [
            pltpu.roll(
                jnp.broadcast_to(lines[i : i + 1, :], (8, LANES)), TASKS, 1, stride=TASKS, stride_axis=0
            )
            for i in range(2)
        ],
        axis=0,
    )
    orders = order_ref[...]
    norm = jnp.sum(jnp.where(row == lane, gram, 0.0), axis=0, keepdims=True)
    norm = jnp.take_along_axis(jnp.broadcast_to(norm, gram.shape), orders, axis=1)
    scale_ref[...] = active_ref[...] / (norm + 1e-06)
    for k in range(TASKS):
        line = jnp.broadcast_to(gram[k : k + 1, :], gram.shape)
        partner_ref[k] = jnp.take_along_axis(line, orders, axis=1)
    full = (8, LANES)
    coef = [jnp.where(lane[:8] == k, 1.0, 0.0) for k in range(TASKS)]
    for s in range(TASKS):
        terms = [coef[k] * jnp.broadcast_to(partner_ref[k, s : s + 1, :], full) for k in range(TASKS)]
        while len(terms) > 1:
            terms = [a + b for a, b in zip(terms[::2], terms[1::2])]
        factor = jnp.broadcast_to(scale_ref[s : s + 1, :], full) * terms[0]
        pick = jnp.broadcast_to(order_ref[s : s + 1, :], full)
        coef = [coef[k] - jnp.where(pick == k, factor, 0.0) for k in range(TASKS)]
    total = None
    for t in range(TASKS):
        weight = jnp.sum(coef[t], axis=1, keepdims=True)[:1]
        term = weight * r_ref[t]
        total = term if total is None else total + term
    tail = total[:, (TILES - 1) * LANES :]
    for part, out in enumerate((down_ref, up_ref)):
        for i in range(4):
            slot = part * 4 + i
            out[0, 8 * i : 8 * i + 8, :LANES] = total[:, slot * LANES : (slot + 1) * LANES]
            piece = pltpu.roll(tail, LANES - slot * TAIL, 1) if slot else tail
            out[0, 8 * i : 8 * i + 8, LANES:] = piece[:, :TAIL]


def per_device(inputs, cotangent, routes, down_factor, up_factor, order, conflict):
    cot = cotangent[0]
    blocks = jax.ShapeDtypeStruct((SHARDS, 8, LANES), F32)
    gram_blocks = jax.ShapeDtypeStruct((TASKS, 2, LANES), F32)
    plan = (
        jax.ShapeDtypeStruct((TASKS, LANES), jnp.int32),
        jax.ShapeDtypeStruct((TASKS, LANES), F32),
    )
    partial = pl.pallas_call(
        encode_kernel,
        out_shape=blocks,
        in_specs=[HBM] * 5,
        out_specs=VMEM,
        scratch_shapes=[
            pltpu.VMEM((LOCAL, TOKENS), BF16),
            pltpu.VMEM((LOCAL, TOKENS), BF16),
            pltpu.VMEM((1, TOKENS), jnp.int32),
            pltpu.VMEM((LOCAL, TOKENS), BF16),
            pltpu.VMEM((LOCAL, TOKENS), BF16),
            pltpu.SemaphoreType.DMA((5,)),
        ],
        compiler_params=pltpu.CompilerParams(vmem_limit_bytes=48 * 1024 * 1024),
    )(*(pltpu.with_memory_space_constraint(a, pltpu.HBM) for a in (inputs, cot, routes, down_factor, up_factor)))
    pieces = lax.all_to_all(partial, "shard", 0, 0)
    mine = call(sum_kernel, blocks)(in_specs=[VMEM])(pieces)
    codes = lax.all_to_all(mine, "shard", 0, 0)
    grads, done = call(
        grad_kernel,
        (
            jax.ShapeDtypeStruct((EXPERTS, 8, TILES * LANES), F32),
            jax.ShapeDtypeStruct((8, LANES), F32),
        ),
    )(in_specs=[VMEM] * 4)(codes, inputs, cot, routes)
    orders, active = call(plan_kernel, plan)(
        in_specs=[VMEM] * 3,
        cost_estimate=pl.CostEstimate(flops=1 << 20, bytes_accessed=1 << 20, transcendentals=0),
    )(order, conflict, done)
    owned = lax.all_to_all(grads, "task", 0, 0)
    gram = pl.pallas_call(
        gram_kernel,
        out_shape=jax.ShapeDtypeStruct((SHARDS, 2, LANES), F32),
        in_specs=[VMEM],
        out_specs=VMEM,
        scratch_shapes=[pltpu.VMEM((TASKS * TASKS, LANES), F32)],
        compiler_params=pltpu.CompilerParams(vmem_limit_bytes=48 * 1024 * 1024),
    )(owned)
    gram = lax.all_to_all(gram, "shard", 0, 0)
    gram = call(sum_kernel, gram_blocks)(in_specs=[VMEM])(gram)
    gram = lax.all_to_all(gram, "task", 0, 0)
    out = jax.ShapeDtypeStruct((1, RANK, LOCAL), F32)
    return pl.pallas_call(
        combine_kernel,
        out_shape=(out, out),
        in_specs=[VMEM] * 4,
        out_specs=(VMEM, VMEM),
        scratch_shapes=[pltpu.VMEM((TASKS, TASKS, LANES), F32), pltpu.VMEM((TASKS, LANES), F32)],
        compiler_params=pltpu.CompilerParams(vmem_limit_bytes=48 * 1024 * 1024),
    )(gram, owned, orders, active)


def solution(mesh):
    placed = (
        P("shard", None),
        P("task", "shard", None),
        P("task", None),
        P("shard", None),
        P("shard", None),
        P(),
        P(),
    )
    return jax.shard_map(
        per_device,
        mesh=mesh,
        in_specs=placed,
        out_specs=(P("task", None, "shard"), P("task", None, "shard")),
        check_vma=False,
    )
```

```python
import functools

import jax
import jax.numpy as jnp
from jax import lax
from jax.experimental import pallas as pl
from jax.experimental.pallas import tpu as pltpu
from jax.sharding import PartitionSpec as P

EXPERTS = 16
RANK = 32
TOKENS = 512
TASKS = 16
SHARDS = 32
LOCAL = 144
BLOCKS = 3
LANES = 128
TAIL = LOCAL - LANES
TILES = 2 * RANK // 8 + 1
VMEM = pl.BlockSpec(memory_space=pltpu.VMEM)
HBM = pl.BlockSpec(memory_space=pltpu.HBM)
F32 = jnp.float32
BF16 = jnp.bfloat16


def call(kernel, out_shapes):
    return functools.partial(
        pl.pallas_call,
        kernel,
        out_shape=out_shapes,
        out_specs=jax.tree.map(lambda _: VMEM, out_shapes),
        compiler_params=pltpu.CompilerParams(vmem_limit_bytes=48 * 1024 * 1024),
    )


def over_features(factor, tokens):
    return lax.dot_general(
        factor, tokens, (((0,), (0,)), ((), ())), preferred_element_type=F32
    )


def lane_columns(square):
    row = lax.broadcasted_iota(jnp.int32, (TASKS, LANES), 0)
    lane = lax.broadcasted_iota(jnp.int32, (TASKS, LANES), 1)
    out = jnp.zeros((TASKS, LANES), square.dtype)
    for s in range(TASKS):
        column = jnp.broadcast_to(square[:, s : s + 1], out.shape)
        line = jnp.sum(jnp.where(row == lane, column, 0), axis=0, keepdims=True)
        out = jnp.where(row == s, line, out)
    return out


def encode_kernel(
    x_hbm,
    c_hbm,
    routes_hbm,
    down_hbm,
    up_hbm,
    out_ref,
    x_ref,
    c_ref,
    routes_ref,
    down_ref,
    up_ref,
    sems,
):
    pairs = (
        (routes_hbm, routes_ref),
        (x_hbm, x_ref),
        (down_hbm, down_ref),
        (c_hbm, c_ref),
        (up_hbm, up_ref),
    )
    copies = []
    for i, (src, dst) in enumerate(pairs):
        parts = BLOCKS if i else 1
        rows = src.shape[0] // parts
        copies.append(
            [
                pltpu.make_async_copy(
                    src.at[pl.ds(p * rows, rows)], dst.at[pl.ds(p * rows, rows)], sems.at[i, p]
                )
                for p in range(parts)
            ]
        )
        for copy in copies[-1]:
            copy.start()
    copies[0][0].wait()
    route = routes_ref[...]
    for part, (tokens, factor) in enumerate(((x_ref, down_ref), (c_ref, up_ref))):
        for copy in copies[1 + 2 * part] + copies[2 + 2 * part]:
            copy.wait()
        full = over_features(factor[...], tokens[...])
        picked = jnp.zeros((RANK, TOKENS), F32)
        for e in range(EXPERTS):
            picked = picked + jnp.where(route == e, full[e * RANK : (e + 1) * RANK, :], 0.0)
        for i in range(4):
            for q in range(4):
                out_ref[part * 16 + i * 4 + q] = picked[8 * i : 8 * i + 8, q * LANES : (q + 1) * LANES]


def sum_kernel(y_ref, out_ref):
    total = y_ref[0]
    for s in range(1, y_ref.shape[0]):
        total = total + y_ref[s]
    out_ref[...] = jnp.broadcast_to(total[None], out_ref.shape)


def prepare(order_ref, conflict_ref, order_out, active_out):
    row = lax.broadcasted_iota(jnp.int32, (TASKS, LANES), 0)
    lane = lax.broadcasted_iota(jnp.int32, (TASKS, LANES), 1)
    orders = lane_columns(order_ref[...])
    conflicts = jnp.where(row == lane, 0, lane_columns(conflict_ref[...]))
    active = jnp.zeros((TASKS, LANES), jnp.int32)
    for j in range(TASKS):
        active = jnp.where(orders == j, conflicts[j : j + 1, :], active)
    order_out[...] = orders
    active_out[...] = jnp.where(lane < TASKS, active, 0).astype(F32)


def grad_kernel(y_ref, x_ref, c_ref, routes_ref, order_ref, conflict_ref, out_ref, order_out, active_out):
    prepare(order_ref, conflict_ref, order_out, active_out)
    route = jnp.broadcast_to(routes_ref[...], (RANK, TOKENS))
    onehot = [jnp.where(route == e, 1.0, 0.0).astype(BF16) for e in range(EXPERTS)]
    pad = jnp.zeros((2 * LANES - LOCAL, TOKENS), BF16)
    for part, tokens in enumerate((c_ref, x_ref)):
        values = 2.0 * jnp.concatenate(
            [
                jnp.concatenate([y_ref[part * 16 + i * 4 + q] for q in range(4)], axis=1)
                for i in range(4)
            ],
            axis=0,
        )
        feats = jnp.concatenate([tokens[...], pad], axis=0)
        high = values.astype(BF16)
        low = (values - high.astype(F32)).astype(BF16)
        high = jnp.concatenate([high * hot for hot in onehot], axis=0)
        low = jnp.concatenate([low * hot for hot in onehot], axis=0)
        dims = (((1,), (1,)), ((), ()))
        grad = lax.dot_general(high, feats, dims, preferred_element_type=F32) + lax.dot_general(
            low, feats, dims, preferred_element_type=F32
        )
        first = RANK * (1 - part)
        for e in range(EXPERTS):
            tail = jnp.zeros((8, LANES), F32)
            for i in range(4):
                slot = first // 8 + i
                rows = slice(e * RANK + 8 * i, e * RANK + 8 * i + 8)
                out_ref[e, :, slot * LANES : (slot + 1) * LANES] = grad[rows, :LANES]
                piece = grad[rows, LANES:]
                tail = tail + (pltpu.roll(piece, slot * TAIL, 1) if slot else piece)
            if part == 0:
                out_ref[e, :, (TILES - 1) * LANES :] = tail
            else:
                out_ref[e, :, (TILES - 1) * LANES :] += tail


def gram_row(t, u):
    at = t // 8 * LANES + (7 - t % 8) * TASKS + u
    return slice(at, at + 1)


def gram_kernel(r_ref, out_ref, rows_ref):
    for t in range(TASKS):
        mine = [r_ref[t, :, k * LANES : (k + 1) * LANES] for k in range(TILES)]
        for u in range(t, TASKS):
            dot = mine[0] * r_ref[u, :, :LANES]
            for k in range(1, TILES):
                dot = dot + mine[k] * r_ref[u, :, k * LANES : (k + 1) * LANES]
            dot = jnp.sum(dot, axis=0, keepdims=True)
            rows_ref[gram_row(t, u)] = dot
            if u > t:
                rows_ref[gram_row(u, t)] = dot
    rest = rows_ref[...]
    lines = jnp.zeros((8, 2 * LANES), F32)
    for _ in range(3):
        piece = rest.astype(BF16)
        rest = rest - piece.astype(F32)
        lines = lines + lax.dot_general(
            jnp.ones((8, LANES), BF16), piece, (((1,), (1,)), ((), ())), preferred_element_type=F32
        )
    for half in range(2):
        line = lines[:1, half * LANES : (half + 1) * LANES]
        out_ref[:, half : half + 1, :] = jnp.broadcast_to(line[None], (SHARDS, 1, LANES))


def combine_kernel(g_ref, r_ref, order_ref, active_ref, down_ref, up_ref, partner_ref, scale_ref):
    row = lax.broadcasted_iota(jnp.int32, (TASKS, LANES), 0)
    lane = lax.broadcasted_iota(jnp.int32, (TASKS, LANES), 1)
    lines = g_ref[0]
    for t in range(1, TASKS):
        lines = lines + g_ref[t]
    gram = jnp.concatenate(
        [
            pltpu.roll(
                jnp.broadcast_to(lines[i : i + 1, :], (8, LANES)), TASKS, 1, stride=TASKS, stride_axis=0
            )
            for i in range(2)
        ],
        axis=0,
    )
    orders = order_ref[...]
    norm = jnp.sum(jnp.where(row == lane, gram, 0.0), axis=0, keepdims=True)
    norm = jnp.take_along_axis(jnp.broadcast_to(norm, gram.shape), orders, axis=1)
    scale_ref[...] = active_ref[...] / (norm + 1e-06)
    for k in range(TASKS):
        line = jnp.broadcast_to(gram[k : k + 1, :], gram.shape)
        partner_ref[k] = jnp.take_along_axis(line, orders, axis=1)
    full = (8, LANES)
    coef = [jnp.where(lane[:8] == k, 1.0, 0.0) for k in range(TASKS)]
    for s in range(TASKS):
        terms = [coef[k] * jnp.broadcast_to(partner_ref[k, s : s + 1, :], full) for k in range(TASKS)]
        while len(terms) > 1:
            terms = [a + b for a, b in zip(terms[::2], terms[1::2])]
        factor = jnp.broadcast_to(scale_ref[s : s + 1, :], full) * terms[0]
        pick = jnp.broadcast_to(order_ref[s : s + 1, :], full)
        coef = [coef[k] - jnp.where(pick == k, factor, 0.0) for k in range(TASKS)]
    total = None
    for t in range(TASKS):
        weight = jnp.sum(coef[t], axis=1, keepdims=True)[:1]
        term = weight * r_ref[t]
        total = term if total is None else total + term
    tail = total[:, (TILES - 1) * LANES :]
    for part, out in enumerate((down_ref, up_ref)):
        for i in range(4):
            slot = part * 4 + i
            out[0, 8 * i : 8 * i + 8, :LANES] = total[:, slot * LANES : (slot + 1) * LANES]
            piece = pltpu.roll(tail, LANES - slot * TAIL, 1) if slot else tail
            out[0, 8 * i : 8 * i + 8, LANES:] = piece[:, :TAIL]


def per_device(inputs, cotangent, routes, down_factor, up_factor, order, conflict):
    cot = cotangent[0]
    blocks = jax.ShapeDtypeStruct((SHARDS, 8, LANES), F32)
    gram_blocks = jax.ShapeDtypeStruct((TASKS, 2, LANES), F32)
    plan = (
        jax.ShapeDtypeStruct((TASKS, LANES), jnp.int32),
        jax.ShapeDtypeStruct((TASKS, LANES), F32),
    )
    partial = pl.pallas_call(
        encode_kernel,
        out_shape=blocks,
        in_specs=[HBM] * 5,
        out_specs=VMEM,
        scratch_shapes=[
            pltpu.VMEM((LOCAL, TOKENS), BF16),
            pltpu.VMEM((LOCAL, TOKENS), BF16),
            pltpu.VMEM((1, TOKENS), jnp.int32),
            pltpu.VMEM((LOCAL, TOKENS), BF16),
            pltpu.VMEM((LOCAL, TOKENS), BF16),
            pltpu.SemaphoreType.DMA((5, BLOCKS)),
        ],
        compiler_params=pltpu.CompilerParams(vmem_limit_bytes=48 * 1024 * 1024),
    )(*(pltpu.with_memory_space_constraint(a, pltpu.HBM) for a in (inputs, cot, routes, down_factor, up_factor)))
    pieces = lax.all_to_all(partial, "shard", 0, 0)
    mine = call(sum_kernel, blocks)(in_specs=[VMEM])(pieces)
    codes = lax.all_to_all(mine, "shard", 0, 0)
    grads, orders, active = call(
        grad_kernel, (jax.ShapeDtypeStruct((EXPERTS, 8, TILES * LANES), F32), *plan)
    )(in_specs=[VMEM] * 6)(codes, inputs, cot, routes, order, conflict)
    owned = lax.all_to_all(grads, "task", 0, 0)
    gram = pl.pallas_call(
        gram_kernel,
        out_shape=jax.ShapeDtypeStruct((SHARDS, 2, LANES), F32),
        in_specs=[VMEM],
        out_specs=VMEM,
        scratch_shapes=[pltpu.VMEM((TASKS * TASKS, LANES), F32)],
        compiler_params=pltpu.CompilerParams(vmem_limit_bytes=48 * 1024 * 1024),
    )(owned)
    gram = lax.all_to_all(gram, "shard", 0, 0)
    gram = call(sum_kernel, gram_blocks)(in_specs=[VMEM])(gram)
    gram = lax.all_to_all(gram, "task", 0, 0)
    out = jax.ShapeDtypeStruct((1, RANK, LOCAL), F32)
    return pl.pallas_call(
        combine_kernel,
        out_shape=(out, out),
        in_specs=[VMEM] * 4,
        out_specs=(VMEM, VMEM),
        scratch_shapes=[pltpu.VMEM((TASKS, TASKS, LANES), F32), pltpu.VMEM((TASKS, LANES), F32)],
        compiler_params=pltpu.CompilerParams(vmem_limit_bytes=48 * 1024 * 1024),
    )(gram, owned, orders, active)


def solution(mesh):
    placed = (
        P("shard", None),
        P("task", "shard", None),
        P("task", None),
        P("shard", None),
        P("shard", None),
        P(),
        P(),
    )
    return jax.shard_map(
        per_device,
        mesh=mesh,
        in_specs=placed,
        out_specs=(P("task", None, "shard"), P("task", None, "shard")),
        check_vma=False,
    )
```

```python
import functools

import jax
import jax.numpy as jnp
from jax import lax
from jax.experimental import pallas as pl
from jax.experimental.pallas import tpu as pltpu
from jax.sharding import Mesh
from jax.sharding import PartitionSpec as P

EXPERTS = 16
RANK = 32
TOKENS = 512
TASKS = 16
SHARDS = 32
SIDE = 4
SHARD = ("x", "y", "core")
LOCAL = 144
BLOCKS = 3
LANES = 128
TAIL = LOCAL - LANES
TILES = 2 * RANK // 8 + 1
VMEM = pl.BlockSpec(memory_space=pltpu.VMEM)
HBM = pl.BlockSpec(memory_space=pltpu.HBM)
F32 = jnp.float32
BF16 = jnp.bfloat16


def call(kernel, out_shapes):
    return functools.partial(
        pl.pallas_call,
        kernel,
        out_shape=out_shapes,
        out_specs=jax.tree.map(lambda _: VMEM, out_shapes),
        compiler_params=pltpu.CompilerParams(vmem_limit_bytes=48 * 1024 * 1024),
    )


def over_features(factor, tokens):
    return lax.dot_general(
        factor, tokens, (((0,), (0,)), ((), ())), preferred_element_type=F32
    )


def lane_columns(square):
    row = lax.broadcasted_iota(jnp.int32, (TASKS, LANES), 0)
    lane = lax.broadcasted_iota(jnp.int32, (TASKS, LANES), 1)
    out = jnp.zeros((TASKS, LANES), square.dtype)
    for s in range(TASKS):
        column = jnp.broadcast_to(square[:, s : s + 1], out.shape)
        line = jnp.sum(jnp.where(row == lane, column, 0), axis=0, keepdims=True)
        out = jnp.where(row == s, line, out)
    return out


def encode_kernel(
    x_hbm,
    c_hbm,
    routes_hbm,
    down_hbm,
    up_hbm,
    out_ref,
    x_ref,
    c_ref,
    routes_ref,
    down_ref,
    up_ref,
    sems,
):
    pairs = (
        (routes_hbm, routes_ref),
        (x_hbm, x_ref),
        (down_hbm, down_ref),
        (c_hbm, c_ref),
        (up_hbm, up_ref),
    )
    copies = []
    for i, (src, dst) in enumerate(pairs):
        parts = BLOCKS if i else 1
        rows = src.shape[0] // parts
        copies.append(
            [
                pltpu.make_async_copy(
                    src.at[pl.ds(p * rows, rows)], dst.at[pl.ds(p * rows, rows)], sems.at[i, p]
                )
                for p in range(parts)
            ]
        )
        for copy in copies[-1]:
            copy.start()
    copies[0][0].wait()
    route = routes_ref[...]
    for part, (tokens, factor) in enumerate(((x_ref, down_ref), (c_ref, up_ref))):
        for copy in copies[1 + 2 * part] + copies[2 + 2 * part]:
            copy.wait()
        full = over_features(factor[...], tokens[...])
        picked = jnp.zeros((RANK, TOKENS), F32)
        for e in range(EXPERTS):
            picked = picked + jnp.where(route == e, full[e * RANK : (e + 1) * RANK, :], 0.0)
        for i in range(4):
            for q in range(4):
                out_ref[part * 16 + i * 4 + q] = picked[8 * i : 8 * i + 8, q * LANES : (q + 1) * LANES]


def sum_kernel(y_ref, out_ref):
    total = y_ref[0]
    for s in range(1, y_ref.shape[0]):
        total = total + y_ref[s]
    out_ref[...] = jnp.broadcast_to(total[None], out_ref.shape)


def prepare(order_ref, conflict_ref, order_out, active_out):
    row = lax.broadcasted_iota(jnp.int32, (TASKS, LANES), 0)
    lane = lax.broadcasted_iota(jnp.int32, (TASKS, LANES), 1)
    orders = lane_columns(order_ref[...])
    conflicts = jnp.where(row == lane, 0, lane_columns(conflict_ref[...]))
    active = jnp.zeros((TASKS, LANES), jnp.int32)
    for j in range(TASKS):
        active = jnp.where(orders == j, conflicts[j : j + 1, :], active)
    order_out[...] = orders
    active_out[...] = jnp.where(lane < TASKS, active, 0).astype(F32)


def grad_kernel(y_ref, x_ref, c_ref, routes_ref, order_ref, conflict_ref, out_ref, order_out, active_out):
    prepare(order_ref, conflict_ref, order_out, active_out)
    route = jnp.broadcast_to(routes_ref[...], (RANK, TOKENS))
    onehot = [jnp.where(route == e, 1.0, 0.0).astype(BF16) for e in range(EXPERTS)]
    pad = jnp.zeros((2 * LANES - LOCAL, TOKENS), BF16)
    for part, tokens in enumerate((c_ref, x_ref)):
        values = 2.0 * jnp.concatenate(
            [
                jnp.concatenate([y_ref[part * 16 + i * 4 + q] for q in range(4)], axis=1)
                for i in range(4)
            ],
            axis=0,
        )
        feats = jnp.concatenate([tokens[...], pad], axis=0)
        high = values.astype(BF16)
        low = (values - high.astype(F32)).astype(BF16)
        high = jnp.concatenate([high * hot for hot in onehot], axis=0)
        low = jnp.concatenate([low * hot for hot in onehot], axis=0)
        dims = (((1,), (1,)), ((), ()))
        grad = lax.dot_general(high, feats, dims, preferred_element_type=F32) + lax.dot_general(
            low, feats, dims, preferred_element_type=F32
        )
        first = RANK * (1 - part)
        for e in range(EXPERTS):
            tail = jnp.zeros((8, LANES), F32)
            for i in range(4):
                slot = first // 8 + i
                rows = slice(e * RANK + 8 * i, e * RANK + 8 * i + 8)
                out_ref[e, :, slot * LANES : (slot + 1) * LANES] = grad[rows, :LANES]
                piece = grad[rows, LANES:]
                tail = tail + (pltpu.roll(piece, slot * TAIL, 1) if slot else piece)
            if part == 0:
                out_ref[e, :, (TILES - 1) * LANES :] = tail
            else:
                out_ref[e, :, (TILES - 1) * LANES :] += tail


def gram_row(t, u):
    at = t // 8 * LANES + (7 - t % 8) * TASKS + u
    return slice(at, at + 1)


def gram_kernel(r_ref, out_ref, rows_ref):
    for t in range(TASKS):
        mine = [r_ref[t, :, k * LANES : (k + 1) * LANES] for k in range(TILES)]
        for u in range(t, TASKS):
            dot = mine[0] * r_ref[u, :, :LANES]
            for k in range(1, TILES):
                dot = dot + mine[k] * r_ref[u, :, k * LANES : (k + 1) * LANES]
            dot = jnp.sum(dot, axis=0, keepdims=True)
            rows_ref[gram_row(t, u)] = dot
            if u > t:
                rows_ref[gram_row(u, t)] = dot
    rest = rows_ref[...]
    lines = jnp.zeros((8, 2 * LANES), F32)
    for _ in range(3):
        piece = rest.astype(BF16)
        rest = rest - piece.astype(F32)
        lines = lines + lax.dot_general(
            jnp.ones((8, LANES), BF16), piece, (((1,), (1,)), ((), ())), preferred_element_type=F32
        )
    for half in range(2):
        line = lines[:1, half * LANES : (half + 1) * LANES]
        out_ref[:, half : half + 1, :] = jnp.broadcast_to(line[None], (SHARDS // SIDE, 1, LANES))


def combine_kernel(g_ref, r_ref, order_ref, active_ref, down_ref, up_ref, partner_ref, scale_ref):
    row = lax.broadcasted_iota(jnp.int32, (TASKS, LANES), 0)
    lane = lax.broadcasted_iota(jnp.int32, (TASKS, LANES), 1)
    lines = g_ref[0]
    for t in range(1, g_ref.shape[0]):
        lines = lines + g_ref[t]
    gram = jnp.concatenate(
        [
            pltpu.roll(
                jnp.broadcast_to(lines[i : i + 1, :], (8, LANES)), TASKS, 1, stride=TASKS, stride_axis=0
            )
            for i in range(2)
        ],
        axis=0,
    )
    orders = order_ref[...]
    norm = jnp.sum(jnp.where(row == lane, gram, 0.0), axis=0, keepdims=True)
    norm = jnp.take_along_axis(jnp.broadcast_to(norm, gram.shape), orders, axis=1)
    scale_ref[...] = active_ref[...] / (norm + 1e-06)
    for k in range(TASKS):
        line = jnp.broadcast_to(gram[k : k + 1, :], gram.shape)
        partner_ref[k] = jnp.take_along_axis(line, orders, axis=1)
    full = (8, LANES)
    coef = [jnp.where(lane[:8] == k, 1.0, 0.0) for k in range(TASKS)]
    for s in range(TASKS):
        terms = [coef[k] * jnp.broadcast_to(partner_ref[k, s : s + 1, :], full) for k in range(TASKS)]
        while len(terms) > 1:
            terms = [a + b for a, b in zip(terms[::2], terms[1::2])]
        factor = jnp.broadcast_to(scale_ref[s : s + 1, :], full) * terms[0]
        pick = jnp.broadcast_to(order_ref[s : s + 1, :], full)
        coef = [coef[k] - jnp.where(pick == k, factor, 0.0) for k in range(TASKS)]
    total = None
    for t in range(TASKS):
        weight = jnp.sum(coef[t], axis=1, keepdims=True)[:1]
        term = weight * r_ref[t]
        total = term if total is None else total + term
    tail = total[:, (TILES - 1) * LANES :]
    for part, out in enumerate((down_ref, up_ref)):
        for i in range(4):
            slot = part * 4 + i
            out[0, 8 * i : 8 * i + 8, :LANES] = total[:, slot * LANES : (slot + 1) * LANES]
            piece = pltpu.roll(tail, LANES - slot * TAIL, 1) if slot else tail
            out[0, 8 * i : 8 * i + 8, LANES:] = piece[:, :TAIL]


def per_device(inputs, cotangent, routes, down_factor, up_factor, order, conflict):
    cot = cotangent[0]
    blocks = jax.ShapeDtypeStruct((SHARDS, 8, LANES), F32)
    gram_blocks = jax.ShapeDtypeStruct((TASKS * SIDE, 2, LANES), F32)
    plan = (
        jax.ShapeDtypeStruct((TASKS, LANES), jnp.int32),
        jax.ShapeDtypeStruct((TASKS, LANES), F32),
    )
    partial = pl.pallas_call(
        encode_kernel,
        out_shape=blocks,
        in_specs=[HBM] * 5,
        out_specs=VMEM,
        scratch_shapes=[
            pltpu.VMEM((LOCAL, TOKENS), BF16),
            pltpu.VMEM((LOCAL, TOKENS), BF16),
            pltpu.VMEM((1, TOKENS), jnp.int32),
            pltpu.VMEM((LOCAL, TOKENS), BF16),
            pltpu.VMEM((LOCAL, TOKENS), BF16),
            pltpu.SemaphoreType.DMA((5, BLOCKS)),
        ],
        compiler_params=pltpu.CompilerParams(vmem_limit_bytes=48 * 1024 * 1024),
    )(*(pltpu.with_memory_space_constraint(a, pltpu.HBM) for a in (inputs, cot, routes, down_factor, up_factor)))
    pieces = lax.all_to_all(partial, SHARD, 0, 0)
    mine = call(sum_kernel, blocks)(in_specs=[VMEM])(pieces)
    codes = lax.all_to_all(mine, SHARD, 0, 0)
    grads, orders, active = call(
        grad_kernel, (jax.ShapeDtypeStruct((EXPERTS, 8, TILES * LANES), F32), *plan)
    )(in_specs=[VMEM] * 6)(codes, inputs, cot, routes, order, conflict)
    owned = lax.all_to_all(grads, "task", 0, 0)
    gram = pl.pallas_call(
        gram_kernel,
        out_shape=jax.ShapeDtypeStruct((SHARDS // SIDE, 2, LANES), F32),
        in_specs=[VMEM],
        out_specs=VMEM,
        scratch_shapes=[pltpu.VMEM((TASKS * TASKS, LANES), F32)],
        compiler_params=pltpu.CompilerParams(vmem_limit_bytes=48 * 1024 * 1024),
    )(owned)
    gram = lax.all_to_all(gram, ("x", "core"), 0, 0)
    gram = call(sum_kernel, gram_blocks)(in_specs=[VMEM])(gram)
    gram = lax.all_to_all(gram, ("task", "y"), 0, 0)
    out = jax.ShapeDtypeStruct((1, RANK, LOCAL), F32)
    return pl.pallas_call(
        combine_kernel,
        out_shape=(out, out),
        in_specs=[VMEM] * 4,
        out_specs=(VMEM, VMEM),
        scratch_shapes=[pltpu.VMEM((TASKS, TASKS, LANES), F32), pltpu.VMEM((TASKS, LANES), F32)],
        compiler_params=pltpu.CompilerParams(vmem_limit_bytes=48 * 1024 * 1024),
    )(gram, owned, orders, active)


def solution(mesh):
    mesh = Mesh(mesh.devices.reshape(TASKS, SIDE, SIDE, 2), ("task", *SHARD))
    placed = (
        P(SHARD, None),
        P("task", SHARD, None),
        P("task", None),
        P(SHARD, None),
        P(SHARD, None),
        P(),
        P(),
    )
    return jax.shard_map(
        per_device,
        mesh=mesh,
        in_specs=placed,
        out_specs=(P("task", None, SHARD), P("task", None, SHARD)),
        check_vma=False,
    )
```

```python
import functools

import jax
import jax.numpy as jnp
from jax import lax
from jax.experimental import pallas as pl
from jax.experimental.pallas import tpu as pltpu
from jax.sharding import PartitionSpec as P

EXPERTS = 16
RANK = 32
TOKENS = 512
TASKS = 16
SHARDS = 32
LOCAL = 144
BLOCKS = 3
LANES = 128
TAIL = LOCAL - LANES
TILES = 2 * RANK // 8 + 1
VMEM = pl.BlockSpec(memory_space=pltpu.VMEM)
HBM = pl.BlockSpec(memory_space=pltpu.HBM)
F32 = jnp.float32
BF16 = jnp.bfloat16


def call(kernel, out_shapes):
    return functools.partial(
        pl.pallas_call,
        kernel,
        out_shape=out_shapes,
        out_specs=jax.tree.map(lambda _: VMEM, out_shapes),
        compiler_params=pltpu.CompilerParams(vmem_limit_bytes=48 * 1024 * 1024),
    )


def over_features(factor, tokens):
    return lax.dot_general(
        factor, tokens, (((0,), (0,)), ((), ())), preferred_element_type=F32
    )


def lane_columns(square):
    row = lax.broadcasted_iota(jnp.int32, (TASKS, LANES), 0)
    lane = lax.broadcasted_iota(jnp.int32, (TASKS, LANES), 1)
    out = jnp.zeros((TASKS, LANES), square.dtype)
    for s in range(TASKS):
        column = jnp.broadcast_to(square[:, s : s + 1], out.shape)
        line = jnp.sum(jnp.where(row == lane, column, 0), axis=0, keepdims=True)
        out = jnp.where(row == s, line, out)
    return out


def encode_kernel(
    x_hbm,
    c_hbm,
    routes_hbm,
    down_hbm,
    up_hbm,
    out_ref,
    x_ref,
    c_ref,
    routes_ref,
    down_ref,
    up_ref,
    sems,
):
    pairs = (
        (routes_hbm, routes_ref),
        (x_hbm, x_ref),
        (down_hbm, down_ref),
        (c_hbm, c_ref),
        (up_hbm, up_ref),
    )
    copies = []
    for i, (src, dst) in enumerate(pairs):
        parts = BLOCKS if i else 1
        rows = src.shape[0] // parts
        copies.append(
            [
                pltpu.make_async_copy(
                    src.at[pl.ds(p * rows, rows)], dst.at[pl.ds(p * rows, rows)], sems.at[i, p]
                )
                for p in range(parts)
            ]
        )
        for copy in copies[-1]:
            copy.start()
    copies[0][0].wait()
    route = routes_ref[...]
    for part, (tokens, factor) in enumerate(((x_ref, down_ref), (c_ref, up_ref))):
        for copy in copies[1 + 2 * part] + copies[2 + 2 * part]:
            copy.wait()
        full = over_features(factor[...], tokens[...])
        picked = jnp.zeros((RANK, TOKENS), F32)
        for e in range(EXPERTS):
            picked = picked + jnp.where(route == e, full[e * RANK : (e + 1) * RANK, :], 0.0)
        for i in range(4):
            for q in range(4):
                out_ref[part * 16 + i * 4 + q] = picked[8 * i : 8 * i + 8, q * LANES : (q + 1) * LANES]


def sum_kernel(y_ref, out_ref):
    total = y_ref[0]
    for s in range(1, y_ref.shape[0]):
        total = total + y_ref[s]
    out_ref[...] = jnp.broadcast_to(total[None], out_ref.shape)


def prepare(order_ref, conflict_ref, order_out, active_out):
    row = lax.broadcasted_iota(jnp.int32, (TASKS, LANES), 0)
    lane = lax.broadcasted_iota(jnp.int32, (TASKS, LANES), 1)
    orders = lane_columns(order_ref[...])
    conflicts = jnp.where(row == lane, 0, lane_columns(conflict_ref[...]))
    active = jnp.zeros((TASKS, LANES), jnp.int32)
    for j in range(TASKS):
        active = jnp.where(orders == j, conflicts[j : j + 1, :], active)
    order_out[...] = orders
    active_out[...] = jnp.where(lane < TASKS, active, 0).astype(F32)


def grad_kernel(y_ref, x_ref, c_ref, routes_ref, order_ref, conflict_ref, out_ref, order_out, active_out):
    prepare(order_ref, conflict_ref, order_out, active_out)
    route = jnp.broadcast_to(routes_ref[...], (RANK, TOKENS))
    onehot = [jnp.where(route == e, 1.0, 0.0).astype(BF16) for e in range(EXPERTS)]
    pad = jnp.zeros((2 * LANES - LOCAL, TOKENS), BF16)
    for part, tokens in enumerate((c_ref, x_ref)):
        values = 2.0 * jnp.concatenate(
            [
                jnp.concatenate([y_ref[part * 16 + i * 4 + q] for q in range(4)], axis=1)
                for i in range(4)
            ],
            axis=0,
        )
        feats = jnp.concatenate([tokens[...], pad], axis=0)
        high = values.astype(BF16)
        low = (values - high.astype(F32)).astype(BF16)
        high = jnp.concatenate([high * hot for hot in onehot], axis=0)
        low = jnp.concatenate([low * hot for hot in onehot], axis=0)
        dims = (((1,), (1,)), ((), ()))
        grad = lax.dot_general(high, feats, dims, preferred_element_type=F32) + lax.dot_general(
            low, feats, dims, preferred_element_type=F32
        )
        first = RANK * (1 - part)
        for e in range(EXPERTS):
            tail = jnp.zeros((8, LANES), F32)
            for i in range(4):
                slot = first // 8 + i
                rows = slice(e * RANK + 8 * i, e * RANK + 8 * i + 8)
                out_ref[e, :, slot * LANES : (slot + 1) * LANES] = grad[rows, :LANES]
                piece = grad[rows, LANES:]
                tail = tail + (pltpu.roll(piece, slot * TAIL, 1) if slot else piece)
            if part == 0:
                out_ref[e, :, (TILES - 1) * LANES :] = tail
            else:
                out_ref[e, :, (TILES - 1) * LANES :] += tail


def gram_row(t, u):
    at = t // 8 * LANES + (7 - t % 8) * TASKS + u
    return slice(at, at + 1)


def gram_kernel(r_ref, out_ref, rows_ref):
    for t in range(TASKS):
        mine = [r_ref[t, :, k * LANES : (k + 1) * LANES] for k in range(TILES)]
        for u in range(t, TASKS):
            dot = mine[0] * r_ref[u, :, :LANES]
            for k in range(1, TILES):
                dot = dot + mine[k] * r_ref[u, :, k * LANES : (k + 1) * LANES]
            dot = jnp.sum(dot, axis=0, keepdims=True)
            rows_ref[gram_row(t, u)] = dot
            if u > t:
                rows_ref[gram_row(u, t)] = dot
    rest = rows_ref[...]
    lines = jnp.zeros((8, 2 * LANES), F32)
    for _ in range(3):
        piece = rest.astype(BF16)
        rest = rest - piece.astype(F32)
        lines = lines + lax.dot_general(
            jnp.ones((8, LANES), BF16), piece, (((1,), (1,)), ((), ())), preferred_element_type=F32
        )
    for half in range(2):
        line = lines[:1, half * LANES : (half + 1) * LANES]
        out_ref[:, half : half + 1, :] = jnp.broadcast_to(line[None], (SHARDS, 1, LANES))


def combine_kernel(g_ref, r_ref, order_ref, active_ref, down_hbm, up_hbm, down_ref, up_ref, partner_ref, scale_ref, sems):
    row = lax.broadcasted_iota(jnp.int32, (TASKS, LANES), 0)
    lane = lax.broadcasted_iota(jnp.int32, (TASKS, LANES), 1)
    lines = g_ref[0]
    for t in range(1, TASKS):
        lines = lines + g_ref[t]
    gram = jnp.concatenate(
        [
            pltpu.roll(
                jnp.broadcast_to(lines[i : i + 1, :], (8, LANES)), TASKS, 1, stride=TASKS, stride_axis=0
            )
            for i in range(2)
        ],
        axis=0,
    )
    orders = order_ref[...]
    norm = jnp.sum(jnp.where(row == lane, gram, 0.0), axis=0, keepdims=True)
    norm = jnp.take_along_axis(jnp.broadcast_to(norm, gram.shape), orders, axis=1)
    scale_ref[...] = active_ref[...] / (norm + 1e-06)
    for k in range(TASKS):
        line = jnp.broadcast_to(gram[k : k + 1, :], gram.shape)
        partner_ref[k] = jnp.take_along_axis(line, orders, axis=1)
    full = (8, LANES)
    coef = [jnp.where(lane[:8] == k, 1.0, 0.0) for k in range(TASKS)]
    for s in range(TASKS):
        terms = [coef[k] * jnp.broadcast_to(partner_ref[k, s : s + 1, :], full) for k in range(TASKS)]
        while len(terms) > 1:
            terms = [a + b for a, b in zip(terms[::2], terms[1::2])]
        factor = jnp.broadcast_to(scale_ref[s : s + 1, :], full) * terms[0]
        pick = jnp.broadcast_to(order_ref[s : s + 1, :], full)
        coef = [coef[k] - jnp.where(pick == k, factor, 0.0) for k in range(TASKS)]
    weights = [jnp.broadcast_to(jnp.sum(coef[t], axis=1, keepdims=True), full) for t in range(TASKS)]

    def combined(k):
        terms = [weights[t] * r_ref[t, :, k * LANES : (k + 1) * LANES] for t in range(TASKS)]
        while len(terms) > 1:
            terms = [a + b for a, b in zip(terms[::2], terms[1::2])]
        return terms[0]

    tail = combined(TILES - 1)
    copies = []
    for part, (out, hbm) in enumerate(((down_ref, down_hbm), (up_ref, up_hbm))):
        for i in range(4):
            slot = part * 4 + i
            out[0, 8 * i : 8 * i + 8, :LANES] = combined(slot)
            piece = pltpu.roll(tail, LANES - slot * TAIL, 1) if slot else tail
            out[0, 8 * i : 8 * i + 8, LANES:] = piece[:, :TAIL]
        copies.append(pltpu.make_async_copy(out, hbm, sems.at[part]))
        copies[-1].start()
    for copy in copies:
        copy.wait()


def per_device(inputs, cotangent, routes, down_factor, up_factor, order, conflict):
    cot = cotangent[0]
    blocks = jax.ShapeDtypeStruct((SHARDS, 8, LANES), F32)
    gram_blocks = jax.ShapeDtypeStruct((TASKS, 2, LANES), F32)
    plan = (
        jax.ShapeDtypeStruct((TASKS, LANES), jnp.int32),
        jax.ShapeDtypeStruct((TASKS, LANES), F32),
    )
    partial = pl.pallas_call(
        encode_kernel,
        out_shape=blocks,
        in_specs=[HBM] * 5,
        out_specs=VMEM,
        scratch_shapes=[
            pltpu.VMEM((LOCAL, TOKENS), BF16),
            pltpu.VMEM((LOCAL, TOKENS), BF16),
            pltpu.VMEM((1, TOKENS), jnp.int32),
            pltpu.VMEM((LOCAL, TOKENS), BF16),
            pltpu.VMEM((LOCAL, TOKENS), BF16),
            pltpu.SemaphoreType.DMA((5, BLOCKS)),
        ],
        compiler_params=pltpu.CompilerParams(vmem_limit_bytes=48 * 1024 * 1024),
    )(*(pltpu.with_memory_space_constraint(a, pltpu.HBM) for a in (inputs, cot, routes, down_factor, up_factor)))
    pieces = lax.all_to_all(partial, "shard", 0, 0)
    mine = call(sum_kernel, blocks)(in_specs=[VMEM])(pieces)
    codes = lax.all_to_all(mine, "shard", 0, 0)
    grads, orders, active = call(
        grad_kernel, (jax.ShapeDtypeStruct((EXPERTS, 8, TILES * LANES), F32), *plan)
    )(in_specs=[VMEM] * 6)(codes, inputs, cot, routes, order, conflict)
    owned = lax.all_to_all(grads, "task", 0, 0)
    gram = pl.pallas_call(
        gram_kernel,
        out_shape=jax.ShapeDtypeStruct((SHARDS, 2, LANES), F32),
        in_specs=[VMEM],
        out_specs=VMEM,
        scratch_shapes=[pltpu.VMEM((TASKS * TASKS, LANES), F32)],
        compiler_params=pltpu.CompilerParams(vmem_limit_bytes=48 * 1024 * 1024),
    )(owned)
    gram = lax.all_to_all(gram, "shard", 0, 0)
    gram = call(sum_kernel, gram_blocks)(in_specs=[VMEM])(gram)
    gram = lax.all_to_all(gram, "task", 0, 0)
    out = jax.ShapeDtypeStruct((1, RANK, LOCAL), F32)
    return pl.pallas_call(
        combine_kernel,
        out_shape=(out, out),
        in_specs=[VMEM] * 4,
        out_specs=(HBM, HBM),
        scratch_shapes=[
            pltpu.VMEM((1, RANK, LOCAL), F32),
            pltpu.VMEM((1, RANK, LOCAL), F32),
            pltpu.VMEM((TASKS, TASKS, LANES), F32),
            pltpu.VMEM((TASKS, LANES), F32),
            pltpu.SemaphoreType.DMA((2,)),
        ],
        compiler_params=pltpu.CompilerParams(vmem_limit_bytes=48 * 1024 * 1024),
    )(gram, owned, orders, active)


def solution(mesh):
    placed = (
        P("shard", None),
        P("task", "shard", None),
        P("task", None),
        P("shard", None),
        P("shard", None),
        P(),
        P(),
    )
    return jax.shard_map(
        per_device,
        mesh=mesh,
        in_specs=placed,
        out_specs=(P("task", None, "shard"), P("task", None, "shard")),
        check_vma=False,
    )
```

```python
import functools

import jax
import jax.numpy as jnp
from jax import lax
from jax.experimental import pallas as pl
from jax.experimental.pallas import tpu as pltpu
from jax.sharding import PartitionSpec as P

EXPERTS = 16
RANK = 32
TOKENS = 512
TASKS = 16
SHARDS = 32
LOCAL = 144
BLOCKS = 1
LANES = 128
TAIL = LOCAL - LANES
TILES = 2 * RANK // 8 + 1
VMEM = pl.BlockSpec(memory_space=pltpu.VMEM)
HBM = pl.BlockSpec(memory_space=pltpu.HBM)
F32 = jnp.float32
BF16 = jnp.bfloat16


def call(kernel, out_shapes):
    return functools.partial(
        pl.pallas_call,
        kernel,
        out_shape=out_shapes,
        out_specs=jax.tree.map(lambda _: VMEM, out_shapes),
        compiler_params=pltpu.CompilerParams(vmem_limit_bytes=48 * 1024 * 1024),
    )


def over_features(factor, tokens):
    return lax.dot_general(
        factor, tokens, (((0,), (0,)), ((), ())), preferred_element_type=F32
    )


def lane_columns(square):
    row = lax.broadcasted_iota(jnp.int32, (TASKS, LANES), 0)
    lane = lax.broadcasted_iota(jnp.int32, (TASKS, LANES), 1)
    out = jnp.zeros((TASKS, LANES), square.dtype)
    for s in range(TASKS):
        column = jnp.broadcast_to(square[:, s : s + 1], out.shape)
        line = jnp.sum(jnp.where(row == lane, column, 0), axis=0, keepdims=True)
        out = jnp.where(row == s, line, out)
    return out


def encode_kernel(
    x_hbm,
    c_hbm,
    routes_hbm,
    down_hbm,
    up_hbm,
    out_ref,
    x_ref,
    c_ref,
    routes_ref,
    down_ref,
    up_ref,
    sems,
):
    pairs = (
        (routes_hbm, routes_ref),
        (x_hbm, x_ref),
        (down_hbm, down_ref),
        (c_hbm, c_ref),
        (up_hbm, up_ref),
    )
    copies = []
    for i, (src, dst) in enumerate(pairs):
        parts = BLOCKS if i else 1
        rows = src.shape[0] // parts
        copies.append(
            [
                pltpu.make_async_copy(
                    src.at[pl.ds(p * rows, rows)], dst.at[pl.ds(p * rows, rows)], sems.at[i, p]
                )
                for p in range(parts)
            ]
        )
        for copy in copies[-1]:
            copy.start()
    copies[0][0].wait()
    route = routes_ref[...]
    for part, (tokens, factor) in enumerate(((x_ref, down_ref), (c_ref, up_ref))):
        for copy in copies[1 + 2 * part] + copies[2 + 2 * part]:
            copy.wait()
        full = over_features(factor[...], tokens[...])
        picked = jnp.zeros((RANK, TOKENS), F32)
        for e in range(EXPERTS):
            picked = picked + jnp.where(route == e, full[e * RANK : (e + 1) * RANK, :], 0.0)
        for i in range(4):
            for q in range(4):
                out_ref[part * 16 + i * 4 + q] = picked[8 * i : 8 * i + 8, q * LANES : (q + 1) * LANES]


def sum_kernel(y_ref, out_ref):
    total = y_ref[0]
    for s in range(1, y_ref.shape[0]):
        total = total + y_ref[s]
    out_ref[...] = jnp.broadcast_to(total[None], out_ref.shape)


def prepare(order_ref, conflict_ref, order_out, active_out):
    row = lax.broadcasted_iota(jnp.int32, (TASKS, LANES), 0)
    lane = lax.broadcasted_iota(jnp.int32, (TASKS, LANES), 1)
    orders = lane_columns(order_ref[...])
    conflicts = jnp.where(row == lane, 0, lane_columns(conflict_ref[...]))
    active = jnp.zeros((TASKS, LANES), jnp.int32)
    for j in range(TASKS):
        active = jnp.where(orders == j, conflicts[j : j + 1, :], active)
    order_out[...] = orders
    active_out[...] = jnp.where(lane < TASKS, active, 0).astype(F32)


def grad_kernel(y_ref, x_ref, c_ref, routes_ref, order_ref, conflict_ref, out_ref, order_out, active_out):
    prepare(order_ref, conflict_ref, order_out, active_out)
    route = jnp.broadcast_to(routes_ref[...], (RANK, TOKENS))
    onehot = [jnp.where(route == e, 1.0, 0.0).astype(BF16) for e in range(EXPERTS)]
    pad = jnp.zeros((2 * LANES - LOCAL, TOKENS), BF16)
    for part, tokens in enumerate((c_ref, x_ref)):
        values = 2.0 * jnp.concatenate(
            [
                jnp.concatenate([y_ref[part * 16 + i * 4 + q] for q in range(4)], axis=1)
                for i in range(4)
            ],
            axis=0,
        )
        feats = jnp.concatenate([tokens[...], pad], axis=0)
        high = values.astype(BF16)
        low = (values - high.astype(F32)).astype(BF16)
        high = jnp.concatenate([high * hot for hot in onehot], axis=0)
        low = jnp.concatenate([low * hot for hot in onehot], axis=0)
        dims = (((1,), (1,)), ((), ()))
        grad = lax.dot_general(high, feats, dims, preferred_element_type=F32) + lax.dot_general(
            low, feats, dims, preferred_element_type=F32
        )
        first = RANK * (1 - part)
        for e in range(EXPERTS):
            tail = jnp.zeros((8, LANES), F32)
            for i in range(4):
                slot = first // 8 + i
                rows = slice(e * RANK + 8 * i, e * RANK + 8 * i + 8)
                out_ref[e, :, slot * LANES : (slot + 1) * LANES] = grad[rows, :LANES]
                piece = grad[rows, LANES:]
                tail = tail + (pltpu.roll(piece, slot * TAIL, 1) if slot else piece)
            if part == 0:
                out_ref[e, :, (TILES - 1) * LANES :] = tail
            else:
                out_ref[e, :, (TILES - 1) * LANES :] += tail


def gram_row(t, u):
    at = t // 8 * LANES + (7 - t % 8) * TASKS + u
    return slice(at, at + 1)


def gram_kernel(r_ref, out_ref, rows_ref):
    for t in range(TASKS):
        mine = [r_ref[t, :, k * LANES : (k + 1) * LANES] for k in range(TILES)]
        for u in range(t, TASKS):
            dot = mine[0] * r_ref[u, :, :LANES]
            for k in range(1, TILES):
                dot = dot + mine[k] * r_ref[u, :, k * LANES : (k + 1) * LANES]
            dot = jnp.sum(dot, axis=0, keepdims=True)
            rows_ref[gram_row(t, u)] = dot
            if u > t:
                rows_ref[gram_row(u, t)] = dot
    rest = rows_ref[...]
    lines = jnp.zeros((8, 2 * LANES), F32)
    for _ in range(3):
        piece = rest.astype(BF16)
        rest = rest - piece.astype(F32)
        lines = lines + lax.dot_general(
            jnp.ones((8, LANES), BF16), piece, (((1,), (1,)), ((), ())), preferred_element_type=F32
        )
    for half in range(2):
        line = lines[:1, half * LANES : (half + 1) * LANES]
        out_ref[:, half : half + 1, :] = jnp.broadcast_to(line[None], (SHARDS, 1, LANES))


def combine_kernel(g_ref, r_ref, order_ref, active_ref, down_hbm, up_hbm, down_ref, up_ref, partner_ref, scale_ref, sems):
    row = lax.broadcasted_iota(jnp.int32, (TASKS, LANES), 0)
    lane = lax.broadcasted_iota(jnp.int32, (TASKS, LANES), 1)
    lines = g_ref[0]
    for t in range(1, TASKS):
        lines = lines + g_ref[t]
    gram = jnp.concatenate(
        [
            pltpu.roll(
                jnp.broadcast_to(lines[i : i + 1, :], (8, LANES)), TASKS, 1, stride=TASKS, stride_axis=0
            )
            for i in range(2)
        ],
        axis=0,
    )
    orders = order_ref[...]
    norm = jnp.sum(jnp.where(row == lane, gram, 0.0), axis=0, keepdims=True)
    norm = jnp.take_along_axis(jnp.broadcast_to(norm, gram.shape), orders, axis=1)
    scale_ref[...] = active_ref[...] / (norm + 1e-06)
    for k in range(TASKS):
        line = jnp.broadcast_to(gram[k : k + 1, :], gram.shape)
        partner_ref[k] = jnp.take_along_axis(line, orders, axis=1)
    full = (8, LANES)
    coef = [jnp.where(lane[:8] == k, 1.0, 0.0) for k in range(TASKS)]
    for s in range(TASKS):
        terms = [coef[k] * jnp.broadcast_to(partner_ref[k, s : s + 1, :], full) for k in range(TASKS)]
        while len(terms) > 1:
            terms = [a + b for a, b in zip(terms[::2], terms[1::2])]
        factor = jnp.broadcast_to(scale_ref[s : s + 1, :], full) * terms[0]
        pick = jnp.broadcast_to(order_ref[s : s + 1, :], full)
        coef = [coef[k] - jnp.where(pick == k, factor, 0.0) for k in range(TASKS)]
    weights = [jnp.broadcast_to(jnp.sum(coef[t], axis=1, keepdims=True), full) for t in range(TASKS)]

    def combined(k):
        terms = [weights[t] * r_ref[t, :, k * LANES : (k + 1) * LANES] for t in range(TASKS)]
        while len(terms) > 1:
            terms = [a + b for a, b in zip(terms[::2], terms[1::2])]
        return terms[0]

    tail = combined(TILES - 1)
    copies = []
    for part, (out, hbm) in enumerate(((down_ref, down_hbm), (up_ref, up_hbm))):
        for i in range(4):
            slot = part * 4 + i
            out[0, 8 * i : 8 * i + 8, :LANES] = combined(slot)
            piece = pltpu.roll(tail, LANES - slot * TAIL, 1) if slot else tail
            out[0, 8 * i : 8 * i + 8, LANES:] = piece[:, :TAIL]
        copies.append(pltpu.make_async_copy(out, hbm, sems.at[part]))
        copies[-1].start()
    for copy in copies:
        copy.wait()


def per_device(inputs, cotangent, routes, down_factor, up_factor, order, conflict):
    cot = cotangent[0]
    blocks = jax.ShapeDtypeStruct((SHARDS, 8, LANES), F32)
    gram_blocks = jax.ShapeDtypeStruct((TASKS, 2, LANES), F32)
    plan = (
        jax.ShapeDtypeStruct((TASKS, LANES), jnp.int32),
        jax.ShapeDtypeStruct((TASKS, LANES), F32),
    )
    partial = pl.pallas_call(
        encode_kernel,
        out_shape=blocks,
        in_specs=[HBM] * 5,
        out_specs=VMEM,
        scratch_shapes=[
            pltpu.VMEM((LOCAL, TOKENS), BF16),
            pltpu.VMEM((LOCAL, TOKENS), BF16),
            pltpu.VMEM((1, TOKENS), jnp.int32),
            pltpu.VMEM((LOCAL, TOKENS), BF16),
            pltpu.VMEM((LOCAL, TOKENS), BF16),
            pltpu.SemaphoreType.DMA((5, BLOCKS)),
        ],
        compiler_params=pltpu.CompilerParams(vmem_limit_bytes=48 * 1024 * 1024),
    )(*(pltpu.with_memory_space_constraint(a, pltpu.HBM) for a in (inputs, cot, routes, down_factor, up_factor)))
    pieces = lax.all_to_all(partial, "shard", 0, 0)
    mine = call(sum_kernel, blocks)(in_specs=[VMEM])(pieces)
    codes = lax.all_to_all(mine, "shard", 0, 0)
    grads, orders, active = call(
        grad_kernel, (jax.ShapeDtypeStruct((EXPERTS, 8, TILES * LANES), F32), *plan)
    )(in_specs=[VMEM] * 6)(codes, inputs, cot, routes, order, conflict)
    owned = lax.all_to_all(grads, "task", 0, 0)
    gram = pl.pallas_call(
        gram_kernel,
        out_shape=jax.ShapeDtypeStruct((SHARDS, 2, LANES), F32),
        in_specs=[VMEM],
        out_specs=VMEM,
        scratch_shapes=[pltpu.VMEM((TASKS * TASKS, LANES), F32)],
        compiler_params=pltpu.CompilerParams(vmem_limit_bytes=48 * 1024 * 1024),
    )(owned)
    gram = lax.all_to_all(gram, "shard", 0, 0)
    gram = call(sum_kernel, gram_blocks)(in_specs=[VMEM])(gram)
    gram = lax.all_to_all(gram, "task", 0, 0)
    out = jax.ShapeDtypeStruct((1, RANK, LOCAL), F32)
    return pl.pallas_call(
        combine_kernel,
        out_shape=(out, out),
        in_specs=[VMEM] * 4,
        out_specs=(HBM, HBM),
        scratch_shapes=[
            pltpu.VMEM((1, RANK, LOCAL), F32),
            pltpu.VMEM((1, RANK, LOCAL), F32),
            pltpu.VMEM((TASKS, TASKS, LANES), F32),
            pltpu.VMEM((TASKS, LANES), F32),
            pltpu.SemaphoreType.DMA((2,)),
        ],
        compiler_params=pltpu.CompilerParams(vmem_limit_bytes=48 * 1024 * 1024),
    )(gram, owned, orders, active)


def solution(mesh):
    placed = (
        P("shard", None),
        P("task", "shard", None),
        P("task", None),
        P("shard", None),
        P("shard", None),
        P(),
        P(),
    )
    return jax.shard_map(
        per_device,
        mesh=mesh,
        in_specs=placed,
        out_specs=(P("task", None, "shard"), P("task", None, "shard")),
        check_vma=False,
    )
```
